32 devices in a mesh: groups: 2 (over y), stream: 4 (over z), tensor: 2 (over x), sub: 2 (over core).
Axes of the slice: x: 2, y: 2, z: 4, core: 2. Of those that a mesh axis runs over, the one named last changes fastest.
Arguments:
- lm_query: bfloat16 [192, 3584], P(('groups', 'stream', 'sub'), 'tensor'), parts along dimension 0, may hold values from -6 to 6
- lm_cache: bfloat16 [192, 64, 2, 512], P(('groups', 'stream', 'sub'), None, None, 'tensor'), parts along dimension 0, may hold values from -6 to 6
- language_new_pair: bfloat16 [192, 2, 512], P(('groups', 'stream', 'sub'), None, 'tensor'), parts along dimension 0, may hold values from -6 to 6
- lm_lengths: int32 [192], P('groups'), parts along dimension 0, may hold values from 21 to 64, as said below
- lm_resid: bfloat16 [192, 3584], P(('groups', 'stream'), 'sub'), parts along dimension 0, may hold values from -18 to 18
- lm_wo: bfloat16 [3584, 3584], P('tensor', 'sub'), may hold values from -0.09375 to 0.09375
- lm_gain: bfloat16 [3584], P('sub'), may hold values from 0.5 to 1.5
- lm_adapt: bfloat16 [3584, 1024], P('sub', 'tensor'), may hold values from -0.09375 to 0.09375
- det_noise: bfloat16 [192, 30, 1024], P(('groups', 'stream'), None, ('tensor', 'sub')), parts along dimension 0, may hold values from -18 to 18
- det_pending: bfloat16 [192, 29, 1024], P(('groups', 'stream'), None, ('tensor', 'sub')), parts along dimension 0, may hold values from -6 to 6
- det_cache: bfloat16 [8, 24, 60, 2, 1024], P(('groups', 'stream'), None, None, None, ('tensor', 'sub')), parts along dimension 0, may hold values from -6 to 6
- det_qkv: bfloat16 [3, 1024, 1024], P(None, None, ('tensor', 'sub')), may hold values from -0.1875 to 0.1875
- det_out: bfloat16 [1024, 1024], P(('tensor', 'sub')), may hold values from -0.1875 to 0.1875
- det_gain: bfloat16 [1024], replicated, may hold values from 0.5 to 1.5
- complete: int32 [192], P('groups'), parts along dimension 0, may hold values from 0 to 1, as said below
- owner: int32 [192], P('groups'), parts along dimension 0, may hold values from 0 to 3, as said below
- prev_owner: int32 [192], P('groups'), parts along dimension 0, may hold values from 0 to 3, as said below
Outputs:
- lm_hidden: bfloat16 [192, 3584], P(('groups', 'stream'), 'sub'), parts along dimension 0
- new_state: bfloat16 [8, 4, 6, 30, 1024], P(('groups', 'stream'), None, None, None, ('tensor', 'sub')), parts along dimension 0
The draws below stay inside these ranges and needn't reach their ends.
There are 2 independent parts, one for each index of `groups`. The reference program is written for one: setup_inputs(seed, part) draws one part's arguments, and reference() takes and returns one part's arrays. A program takes and returns all parts, laid end to end along the dimension named above; an argument that names none is the same for every part. Nothing has to cross between parts.
Inputs may be any that keep to these rules, and one draw needn't show every extreme that they name: `lm_lengths`: some stream has exactly 64 valid positions. From one stream shard (streams j * 24 to (j + 1) * 24 - 1) at most 6 complete streams have the same owner, and some owner receives exactly 6 from every shard. `owner`: only the owners of complete streams matter. `prev_owner`: every owner holds exactly 24 streams' caches; at most 6 complete streams share one pair of previous and new owner, and for some new owner that many come from every previous owner.
All inputs are finite; a program needn't handle non-finite values.
Results may differ from the reference program's by a relative error of at most 0.006.
Values may be sent and summed in bfloat16 or wider, within the bound.
A program may use at most 128 MiB of HBM per device.

```python
import jax
import jax.numpy as jnp
from jax import lax

D = 3584
QUERY_HEADS = 28
KEY_VALUE_HEADS = 4
HEAD_WIDTH = 128
C = 1024
DH = 16
DHD = 64
SPAN = 30
PAST = 2
CACHE_LENGTH = 64
SLOTS = 6
OWNERS = 4
SHARD_STREAMS = 24
STREAM_COUNT = 96


def routing_tables(base_key):
    base_key = jax.random.fold_in(base_key, 7321)
    k_count, k_full, k_perm, place_subkey, k_token, k_spare = jax.random.split(base_key, 6)
    counts = jax.random.randint(k_count, (OWNERS, OWNERS), 0, SLOTS + 1)
    full_owner = jax.random.randint(k_full, (), 0, OWNERS)
    counts = jnp.where(jnp.arange(OWNERS)[None, :] == full_owner, SLOTS, counts)
    chosen_index = jnp.arange(SLOTS)[None, None, :] < counts[:, :, None]
    perm_keys = jax.random.split(k_perm, OWNERS * SLOTS)
    prev_perm = jax.vmap(lambda subkey: jax.random.permutation(subkey, OWNERS))(perm_keys)
    prev_perm = prev_perm.reshape(OWNERS, SLOTS, OWNERS)
    prev_flat = jnp.transpose(prev_perm, (2, 0, 1)).reshape(OWNERS, SHARD_STREAMS)
    is_valid = chosen_index.reshape(OWNERS, SHARD_STREAMS)
    owner_flat = jnp.broadcast_to(jnp.arange(OWNERS)[None, :, None], (OWNERS, OWNERS, SLOTS)).reshape(OWNERS, SHARD_STREAMS)
    prev_match = jnp.logical_and(is_valid[..., None], prev_flat[..., None] == jnp.arange(OWNERS)[None, None, :])
    prev_load = jnp.sum(prev_match.astype(jnp.int32), axis=(0, 1))
    token_owner = jnp.repeat(jnp.arange(OWNERS), SHARD_STREAMS)
    token_rank = jnp.tile(jnp.arange(SHARD_STREAMS), OWNERS)
    is_used = token_rank < prev_load[token_owner]
    scores = jax.random.randint(k_token, (STREAM_COUNT,), 0, 2 ** 20)
    scores = jnp.where(is_used, 2 ** 21, scores)
    token_order = jnp.argsort(scores, stable=True)
    invalid = jnp.logical_not(is_valid).reshape(-1)
    spare_rank = jnp.cumsum(invalid.astype(jnp.int32)) - 1
    spare_prev = token_owner[token_order[jnp.clip(spare_rank, 0, STREAM_COUNT - 1)]]
    prev_all = jnp.where(invalid, spare_prev, prev_flat.reshape(-1))
    spare_owner = jax.random.randint(k_spare, (STREAM_COUNT,), 0, OWNERS)
    owner_all = jnp.where(invalid, spare_owner, owner_flat.reshape(-1))
    place_keys = jax.random.split(place_subkey, OWNERS)
    places = jax.vmap(lambda subkey: jax.random.permutation(subkey, SHARD_STREAMS))(place_keys)
    target = (jnp.arange(OWNERS)[:, None] * SHARD_STREAMS + places).reshape(-1)
    done_flags = jnp.zeros((STREAM_COUNT,), jnp.int32).at[target].set(is_valid.reshape(-1).astype(jnp.int32))
    owners = jnp.zeros((STREAM_COUNT,), jnp.int32).at[target].set(owner_all.astype(jnp.int32))
    prev_ids = jnp.zeros((STREAM_COUNT,), jnp.int32).at[target].set(prev_all.astype(jnp.int32))
    return (done_flags, owners, prev_ids)


def draw_complete(key, part):
    return routing_tables(key)[0]


def draw_owner(key, part):
    return routing_tables(key)[1]


def draw_prev_owner(key, part):
    return routing_tables(key)[2]


def draw_lm_lengths(key, part):
    length_key = jax.random.fold_in(key, 911)
    k_lengths, k_longest = jax.random.split(length_key, 2)
    lengths = jax.random.randint(k_lengths, (STREAM_COUNT,), CACHE_LENGTH // 3, CACHE_LENGTH + 1)
    longest = jax.random.randint(k_longest, (), 0, STREAM_COUNT)
    return jnp.where(jnp.arange(STREAM_COUNT) == longest, CACHE_LENGTH, lengths).astype(jnp.int32)


def standard_normal(key, shape):
    return jnp.clip(jax.random.normal(key, shape, jnp.float32), -6.0, 6.0)


def column_scale(width):
    position = jnp.arange(width).astype(jnp.float32) / max(width - 1, 1)
    return 0.5 + 2.0 * position


def draw_lm_resid(key, part):
    value_rows = standard_normal(jax.random.fold_in(key, 107), (STREAM_COUNT, D))
    value_rows = value_rows * column_scale(D)[None, :]
    return value_rows.astype(jnp.bfloat16)


def draw_lm_query(key, part):
    value_rows = standard_normal(jax.random.fold_in(key, 101), (STREAM_COUNT, QUERY_HEADS * HEAD_WIDTH))
    return value_rows.astype(jnp.bfloat16)


def draw_lm_cache(key, part):
    value_rows = standard_normal(jax.random.fold_in(key, 102), (STREAM_COUNT, CACHE_LENGTH, 2, KEY_VALUE_HEADS * HEAD_WIDTH))
    return value_rows.astype(jnp.bfloat16)


def draw_det_noise(key, part):
    value_rows = standard_normal(jax.random.fold_in(key, 103), (STREAM_COUNT, SPAN, C))
    value_rows = value_rows * column_scale(C)[None, None, :]
    return value_rows.astype(jnp.bfloat16)


def draw_det_cache(key, part):
    value_rows = standard_normal(jax.random.fold_in(key, 104), (OWNERS, SHARD_STREAMS, PAST * SPAN, 2, C))
    return value_rows.astype(jnp.bfloat16)


def draw_det_qkv(key, part):
    value_rows = standard_normal(jax.random.fold_in(key, 105), (3, C, C)) * C ** (-0.5)
    return value_rows.astype(jnp.bfloat16)


def block_levels(own_key, extent, cuts, low, high):
    level, own = 1.0, jax.random.fold_in(own_key, 6)
    for dim, parts in cuts:
        heights = jnp.exp(jax.random.uniform(jax.random.fold_in(own, dim), (parts,), jnp.float32, low / len(cuts), high / len(cuts)))
        level = level * jnp.repeat(heights, extent[dim] // parts).reshape([-1 if axis == dim else 1 for axis in range(len(extent))])
    return level


def centred(stream_key, dims, scale, reach, cuts=(), kind=jnp.bfloat16):
    entries = jax.random.normal(stream_key, dims, jnp.float32) * scale
    if len(cuts) > 0:
        entries = block_levels(stream_key, dims, cuts, -0.22, 0.18) * entries
    return jnp.clip(entries, min=-reach, max=reach).astype(kind)


def setup_inputs(seed: int = 0, part: int = 0) -> dict:
    key_of = jax.random.split(jax.random.key(seed), 18)
    own_keys = jax.random.split(jax.random.fold_in(key_of[17], part), 18)
    lm_query = draw_lm_query(jax.random.fold_in(jax.random.fold_in(key_of[17], part), 71), part)
    lm_cache = draw_lm_cache(jax.random.fold_in(jax.random.fold_in(key_of[17], part), 71), part)
    language_new_pair = centred(own_keys[2], (STREAM_COUNT, 2, KEY_VALUE_HEADS * HEAD_WIDTH), 1.0, 6.0, ((0, 8), (2, 2)))
    lm_lengths = draw_lm_lengths(jax.random.fold_in(jax.random.fold_in(key_of[17], part), 71), part)
    lm_resid = draw_lm_resid(jax.random.fold_in(jax.random.fold_in(key_of[17], part), 71), part)
    lm_wo = centred(key_of[5], (QUERY_HEADS * HEAD_WIDTH, D), (QUERY_HEADS * HEAD_WIDTH) ** -0.5, 0.09375, ((0, 2), (1, 2)))
    lm_gain = jnp.clip(1.0 + 0.1 * jax.random.normal(key_of[6], (D,), jnp.float32), 0.5, 1.5).astype(jnp.bfloat16)
    lm_adapt = centred(key_of[7], (D, C), D ** -0.5, 0.09375, ((0, 2), (1, 2)))
    det_noise = draw_det_noise(jax.random.fold_in(jax.random.fold_in(key_of[17], part), 71), part)
    det_pending = centred(own_keys[9], (STREAM_COUNT, SPAN - 1, C), 1.0, 6.0, ((0, 4), (2, 4)))
    det_cache = draw_det_cache(jax.random.fold_in(jax.random.fold_in(key_of[17], part), 71), part)
    det_qkv = draw_det_qkv(jax.random.fold_in(key_of[17], 71), part)
    det_out = centred(key_of[12], (C, C), C ** -0.5, 0.1875, ((0, 4),))
    det_gain = jnp.clip(1.0 + 0.1 * jax.random.normal(key_of[13], (C,), jnp.float32), 0.5, 1.5).astype(jnp.bfloat16)
    complete = draw_complete(jax.random.fold_in(jax.random.fold_in(key_of[17], part), 71), part)
    owner = draw_owner(jax.random.fold_in(jax.random.fold_in(key_of[17], part), 71), part)
    prev_owner = draw_prev_owner(jax.random.fold_in(jax.random.fold_in(key_of[17], part), 71), part)
    return dict(lm_query=lm_query, lm_cache=lm_cache, language_new_pair=language_new_pair, lm_lengths=lm_lengths, lm_resid=lm_resid, lm_wo=lm_wo, lm_gain=lm_gain, lm_adapt=lm_adapt, det_noise=det_noise, det_pending=det_pending, det_cache=det_cache, det_qkv=det_qkv, det_out=det_out, det_gain=det_gain, complete=complete, owner=owner, prev_owner=prev_owner)


step_size = 0.5
epsilon = 1e-06

def rounded(value_rows):
    return lax.optimization_barrier(value_rows.astype(jnp.bfloat16)).astype(jnp.float32)

def decode_attention(query, cache, fresh, lengths):
    streams = query.shape[0]
    kv_heads = cache.shape[-1] // HEAD_WIDTH
    mixing_ratio = QUERY_HEADS // KEY_VALUE_HEADS
    queries = query.astype(jnp.float32).reshape(streams, kv_heads, mixing_ratio, HEAD_WIDTH)
    past_keys = cache[:, :, 0, :].astype(jnp.float32).reshape(streams, CACHE_LENGTH, kv_heads, HEAD_WIDTH)
    past_values = cache[:, :, 1, :].astype(jnp.float32).reshape(streams, CACHE_LENGTH, kv_heads, HEAD_WIDTH)
    fresh_key_rows = fresh[:, 0, :].astype(jnp.float32).reshape(streams, kv_heads, HEAD_WIDTH)
    new_values = fresh[:, 1, :].astype(jnp.float32).reshape(streams, kv_heads, HEAD_WIDTH)
    scale = HEAD_WIDTH ** (-0.5)
    past_scores = jnp.einsum('skgd,slkd->skgl', queries, past_keys) * scale
    new_scores = jnp.einsum('skgd,skd->skg', queries, fresh_key_rows) * scale
    visible = (jnp.arange(CACHE_LENGTH)[None, :] < lengths[:, None])[:, None, None, :]
    masked = jnp.where(visible, past_scores, -1e+30)
    top = jnp.maximum(lax.optimization_barrier(jnp.max(masked, axis=-1)), new_scores)
    past_weights = jnp.where(visible, jnp.exp(masked - top[..., None]), 0.0)
    new_weights = jnp.exp(new_scores - top)
    total = lax.optimization_barrier(jnp.sum(past_weights, axis=-1)) + new_weights
    mixed = jnp.einsum('skgl,slkd->skgd', rounded(past_weights), past_values)
    mixed = mixed + rounded(new_weights)[..., None] * new_values[:, :, None, :]
    return (mixed / total[..., None]).reshape(streams, kv_heads * mixing_ratio * HEAD_WIDTH).astype(jnp.bfloat16)

def flow_step(noise, span, cache, live, det_qkv, det_out, det_gain):
    slots = noise.shape[0]
    past_len = cache.shape[1]
    state = noise.astype(jnp.float32) + span.astype(jnp.float32)
    mean_square = lax.optimization_barrier(jnp.mean(state * state, axis=-1, keepdims=True))
    normed = (state * lax.rsqrt(mean_square + epsilon) * det_gain.astype(jnp.float32)).astype(jnp.bfloat16)
    projected = jnp.einsum('ntc,kce->ntke', normed.astype(jnp.float32), det_qkv.astype(jnp.float32)).astype(jnp.bfloat16)
    queries = projected[:, :, 0].astype(jnp.float32).reshape(slots, SPAN, DH, DHD)
    keys = jnp.concatenate([cache[:, :, 0], projected[:, :, 1]], axis=1).astype(jnp.float32)
    value_rows = jnp.concatenate([cache[:, :, 1], projected[:, :, 2]], axis=1).astype(jnp.float32)
    keys = keys.reshape(slots, past_len + SPAN, DH, DHD)
    value_rows = value_rows.reshape(slots, past_len + SPAN, DH, DHD)
    scores = jnp.einsum('nthd,nlhd->nhtl', queries, keys) * DHD ** (-0.5)
    top = lax.optimization_barrier(jnp.max(scores, axis=-1, keepdims=True))
    weights = jnp.exp(scores - top)
    total = lax.optimization_barrier(jnp.sum(weights, axis=-1))
    mixed = jnp.einsum('nhtl,nlhd->nthd', rounded(weights), value_rows)
    mixed = (mixed / jnp.transpose(total, (0, 2, 1))[..., None]).reshape(slots, SPAN, C).astype(jnp.bfloat16)
    mixing = jnp.einsum('ntc,ce->nte', mixed.astype(jnp.float32), det_out.astype(jnp.float32))
    velocity = span.astype(jnp.float32) - noise.astype(jnp.float32) + mixing
    updated = (noise.astype(jnp.float32) + step_size * velocity) * live[:, None, None]
    return updated.astype(jnp.bfloat16)

def exclusive_rank(hot, reduce_axis):
    return lax.optimization_barrier(jnp.sum((jnp.cumsum(hot, axis=reduce_axis) - hot) * hot, axis=-1))

def reference(lm_query, lm_cache, language_new_pair, lm_lengths, lm_resid, lm_wo, lm_gain, lm_adapt, det_noise, det_pending, det_cache, det_qkv, det_out, det_gain, complete, owner, prev_owner):
    attention = decode_attention(lm_query, lm_cache, language_new_pair, lm_lengths)
    mixing = jnp.dot(attention, lm_wo, preferred_element_type=jnp.float32)
    hidden = (lm_resid.astype(jnp.float32) + mixing).astype(jnp.bfloat16)
    hidden_wide = hidden.astype(jnp.float32)
    mean_square = lax.optimization_barrier(jnp.mean(hidden_wide * hidden_wide, axis=-1, keepdims=True))
    normed = (hidden_wide * lax.rsqrt(mean_square + epsilon) * lm_gain.astype(jnp.float32)).astype(jnp.bfloat16)
    cond_new = jnp.dot(normed, lm_adapt, preferred_element_type=jnp.float32).astype(jnp.bfloat16)
    span = jnp.concatenate([det_pending, cond_new[:, None, :]], axis=1)
    done = complete == 1
    owner_range = jnp.arange(OWNERS).astype(jnp.int32)
    owner_hot = jnp.logical_and(owner[:, None] == owner_range[None, :], done[:, None]).astype(jnp.int32)
    by_home = owner_hot.reshape(OWNERS, SHARD_STREAMS, OWNERS)
    home_rank = lax.optimization_barrier(jnp.sum((jnp.cumsum(by_home, axis=1) - by_home).reshape(STREAM_COUNT, OWNERS) * owner_hot, axis=-1))
    prev_hot = (prev_owner[:, None] == owner_range[None, :]).astype(jnp.int32)
    cache_slot = exclusive_rank(prev_hot, 0)
    stream_ids = jnp.arange(STREAM_COUNT).astype(jnp.int32)
    total_slots = OWNERS * OWNERS * SLOTS
    slot_index = (owner * OWNERS + stream_ids // SHARD_STREAMS) * SLOTS + home_rank
    slot_index = jnp.where(done, slot_index, total_slots).astype(jnp.int32)
    stream_of_slot = jnp.full((total_slots,), -1, jnp.int32).at[slot_index].set(stream_ids, mode='drop')
    present = (stream_of_slot >= 0).astype(jnp.float32)
    source = jnp.maximum(stream_of_slot, 0)

    def one_owner(owner_slots):
        sources, live = owner_slots
        return flow_step(det_noise[sources], span[sources], det_cache[prev_owner[sources], cache_slot[sources]], live, det_qkv, det_out, det_gain)
    new_state = lax.map(one_owner, (source.reshape(OWNERS, OWNERS * SLOTS), present.reshape(OWNERS, OWNERS * SLOTS)))
    return (hidden, new_state.reshape(OWNERS, OWNERS, SLOTS, SPAN, C))
```

```python
import functools

import jax
import jax.numpy as jnp
from jax import lax
from jax.experimental import pallas as pl
from jax.experimental.pallas import tpu as pltpu
from jax.sharding import PartitionSpec as P

QUERY_HEADS = 28
KEY_VALUE_HEADS = 4
HEAD_WIDTH = 128
DHD = 64
SLOTS = 6
MESH = pl.DeviceIdType.MESH

step_size = 0.5
epsilon = 1e-06
NEG = -1e30
F32 = jnp.float32
BF16 = jnp.bfloat16


def up(n, m):
    return (n + m - 1) // m * m


def dot_nt(a, b):
    return lax.dot_general(a, b, (((1,), (1,)), ((), ())), preferred_element_type=F32)


def kernel(
    sizes,
    past_len,
    pack_ref, cpack_ref, crow_ref, order_ref, orow_ref, outidx_ref, live_ref,
    state_ref, dcache_ref, q_ref, lmx_ref, newk_ref, newv_ref, bias_ref, resid_ref, gain_ref,
    dgain_ref,
    wo_hbm, adapt_hbm, qkv_hbm, dout_hbm,
    hid_ref, out_ref,
    wo, adapt, qkv, dout,
    stsend, strecv, csend, crecv, att_all, parts, condx, condf, condpack, condsend, condrecv,
    condrf, gath, n29, lg, lgf, a_s, qb, kb, vb, mx, own, osend, orecv, res,
    w_sem, st_s, st_r, ca_s, ca_r, co_s, co_r, at_s, at_r, pa_s, pa_r, cx_s, cx_r,
    g_s, g_r, l_s, l_r, o_s, o_r,
):
    S, T, U = sizes
    NP = T * U
    me = lax.axis_index("stream")
    t_me = lax.axis_index("tensor")
    u_me = lax.axis_index("sub")
    p_me = t_me * U + u_me
    CW = state_ref.shape[2]
    TOK = state_ref.shape[1]
    SL = S * SLOTS
    KV, NS = q_ref.shape[0], q_ref.shape[1]
    NR = att_all.shape[1]
    R = QUERY_HEADS // KEY_VALUE_HEADS
    last = out_ref.shape[1] - 1

    def at_stream(d):
        return {"stream": lax.rem(me + d, S)}

    def at_part(d):
        peer = lax.rem(p_me + d, NP)
        return {"tensor": lax.div(peer, U), "sub": lax.rem(peer, U)}

    def send(src, dst, ss, rs, dev):
        c = pltpu.make_async_remote_copy(
            src_ref=src, dst_ref=dst, send_sem=ss, recv_sem=rs, device_id=dev,
            device_id_type=MESH,
        )
        c.start()
        return c

    loads = []
    for i, (s, d) in enumerate(((wo_hbm, wo), (adapt_hbm, adapt), (qkv_hbm, qkv), (dout_hbm, dout))):
        c = pltpu.make_async_copy(s, d, w_sem.at[i])
        c.start()
        loads.append(c)

    barrier = pltpu.get_barrier_semaphore()
    for d in range(1, S):
        pl.semaphore_signal(barrier, inc=1, device_id=at_stream(d), device_id_type=MESH)
    for d in range(1, NP):
        pl.semaphore_signal(barrier, inc=1, device_id=at_part(d), device_id_type=MESH)

    def pack_state(i, _):
        stsend[i] = state_ref[pack_ref[i]]
        return 0

    lax.fori_loop(0, SL, pack_state, 0)
    pl.semaphore_wait(barrier, S - 1 + NP - 1)
    st_copies = []
    for d in range(1, S):
        o = lax.rem(me + d, S)
        st_copies.append(
            send(stsend.at[pl.ds(o * SLOTS, SLOTS)], strecv.at[pl.ds(me * SLOTS, SLOTS)],
                 st_s.at[d], st_r.at[d], at_stream(d))
        )

    def pack_cache(i, _):
        csend[i] = dcache_ref[cpack_ref[i]]
        return 0

    lax.fori_loop(0, SL, pack_cache, 0)
    ca_copies = [None]
    for d in range(1, S):
        o = lax.rem(me + d, S)
        ca_copies.append(
            send(csend.at[pl.ds(o * SLOTS, SLOTS)], crecv.at[pl.ds(me * SLOTS, SLOTS)],
                 ca_s.at[d], ca_r.at[d], at_stream(d))
        )

    def keep_own(i, _):
        c = me * SLOTS + i
        strecv[c] = stsend[c]
        crecv[c] = csend[c]
        return 0

    lax.fori_loop(0, SLOTS, keep_own, 0)

    scale = HEAD_WIDTH ** (-0.5)
    bias = bias_ref[...]
    if NR > NS:
        att_all[u_me] = jnp.zeros(att_all.shape[1:], BF16)
    for kv in range(KV):
        q = q_ref[kv]
        x = lmx_ref[:, :, kv * HEAD_WIDTH:(kv + 1) * HEAD_WIDTH]
        s = lax.dot_general(q, x, (((2,), (2,)), ((0,), (0,))), preferred_element_type=F32)
        s = s * scale + bias
        s_new = jnp.sum(q.astype(F32) * newk_ref[kv], axis=-1, keepdims=True) * scale
        top = jnp.maximum(jnp.max(s, axis=-1, keepdims=True), s_new)
        w = jnp.exp(s - top)
        w_new = jnp.exp(s_new - top)
        total = jnp.sum(w, axis=-1, keepdims=True) + w_new
        w_rows = w.reshape(NS * 8, w.shape[2])
        w_odd = pltpu.roll(w_rows, 1, 1).astype(BF16).reshape(w.shape)
        o = lax.dot_general(w_odd, x, (((2,), (1,)), ((0,), (0,))), preferred_element_type=F32)
        o = o + w_new.astype(BF16).astype(F32) * newv_ref[kv]
        o = o / total
        for r in range(R):
            col = (kv * R + r) * HEAD_WIDTH
            att_all[u_me, 0:NS, col:col + HEAD_WIDTH] = o[:, r, :].astype(BF16)
    at_copies = []
    for d in range(1, U):
        at_copies.append(
            send(att_all.at[u_me], att_all.at[u_me], at_s.at[d], at_r.at[d],
                 {"sub": lax.rem(u_me + d, U)})
        )
    for c in at_copies:
        c.wait_recv()
    loads[0].wait()
    M = U * NR
    att = att_all[...].reshape(M, att_all.shape[2])
    parts[t_me] = jnp.dot(att, wo[...], preferred_element_type=F32).astype(BF16)
    pa_copies = []
    for d in range(1, T):
        pa_copies.append(
            send(parts.at[t_me], parts.at[t_me], pa_s.at[d], pa_r.at[d],
                 {"tensor": lax.rem(t_me + d, T)})
        )
    for c in st_copies:
        c.wait_recv()

    def arrange(c, _):
        row = strecv[order_ref[c]]
        gath[p_me, c] = row
        n29[pl.ds(c, 1), :] = row.astype(F32)[last:last + 1, :]
        return 0

    lax.fori_loop(0, SL, arrange, 0)
    for c in pa_copies:
        c.wait_recv()
    g_copies = []
    for d in range(1, NP):
        g_copies.append(send(gath.at[p_me], gath.at[p_me], g_s.at[d], g_r.at[d], at_part(d)))
    mixing = parts[0].astype(F32)
    for t in range(1, T):
        mixing = mixing + parts[t].astype(F32)
    hidden = (resid_ref[...].astype(F32) + mixing).astype(BF16)
    hid_ref[...] = hidden
    wide = hidden.astype(F32)
    gained = (wide * gain_ref[...]).astype(BF16)
    loads[1].wait()
    AW = adapt.shape[1]
    condx[u_me, :, 0:AW] = jnp.dot(gained, adapt[...], preferred_element_type=F32)
    condx[u_me, :, AW:AW + 128] = jnp.broadcast_to(
        jnp.sum(wide * wide, axis=-1, keepdims=True), (M, 128)
    )
    cx_copies = []
    for d in range(1, U):
        cx_copies.append(
            send(condx.at[u_me], condx.at[u_me], cx_s.at[d], cx_r.at[d],
                 {"sub": lax.rem(u_me + d, U)})
        )
    condpack[...] = jnp.zeros(condpack.shape, F32)
    for c in cx_copies:
        c.wait_recv()
    mine = pl.ds(pl.multiple_of(u_me * CW, 128), CW)
    acc, sq = condx[0, :, mine], condx[0, :, AW:AW + 128]
    for u in range(1, U):
        acc = acc + condx[u, :, mine]
        sq = sq + condx[u, :, AW:AW + 128]
    inv = lax.rsqrt(sq[:, 0:1] / (hidden.shape[1] * U) + epsilon)
    condf[...] = acc * inv

    def pack_cond(o, _):
        for r in range(SLOTS):
            condpack[pl.ds(o * 16 + r, 1), :] = condf[pl.ds(crow_ref[o * SLOTS + r], 1), :]
        return 0

    lax.fori_loop(0, S, pack_cond, 0)
    condsend[...] = condpack[...].astype(BF16).reshape(condsend.shape)
    co_copies = []
    for d in range(1, S):
        o = lax.rem(me + d, S)
        co_copies.append(
            send(condsend.at[o], condrecv.at[me], co_s.at[d], co_r.at[d], at_stream(d))
        )
    condrecv[me] = condsend[me]
    lgf[...] = jnp.zeros(lgf.shape, F32)
    for c in co_copies:
        c.wait_recv()
    condrf[...] = condrecv[...].astype(F32).reshape(condrf.shape)

    def last_rows(c, _):
        lgf[p_me, pl.ds(c, 1), :] = n29[pl.ds(c, 1), :] + condrf[pl.ds(orow_ref[c], 1), :]
        return 0

    lax.fori_loop(0, SL, last_rows, 0)
    lg[p_me] = lgf[p_me].astype(BF16)
    l_copies = []
    for d in range(1, NP):
        l_copies.append(send(lg.at[p_me], lg.at[p_me], l_s.at[d], l_r.at[d], at_part(d)))
    for c in g_copies:
        c.wait_recv()
    for c in l_copies:
        c.wait_recv()
    lgf[...] = lg[...].astype(F32)

    is_last = lax.broadcasted_iota(jnp.int32, (TOK, CW), 0) == last

    def full_rows(part, c):
        return jnp.where(is_last, lgf[part, pl.ds(c, 1), :], gath[part, c].astype(F32))

    def normalize(c, _):
        rows = [full_rows(pt, c) for pt in range(NP)]
        ss = rows[0] * rows[0]
        for x in rows[1:]:
            ss = ss + x * x
        inv = lax.rsqrt(jnp.sum(ss, axis=-1, keepdims=True) / (NP * CW) + epsilon)
        for pt in range(NP):
            a_s[c, :, pt * CW:(pt + 1) * CW] = (
                rows[pt] * inv * dgain_ref[:, pt * CW:(pt + 1) * CW]
            ).astype(BF16)
        return 0

    lax.fori_loop(0, SL, normalize, 0)
    loads[2].wait()
    loads[3].wait()

    def project(p, _):
        here = pl.ds(p * SLOTS, SLOTS)
        a = a_s[here].reshape(SLOTS * TOK, NP * CW)
        for k, dst in enumerate((qb, kb, vb)):
            y = jnp.dot(a, qkv[k], preferred_element_type=F32)
            if k == 0:
                y = y * (DHD ** (-0.5))
            dst[here] = y.astype(BF16).reshape(SLOTS, TOK, CW)
        return 0

    lax.fori_loop(0, S, project, 0)

    H = CW // DHD
    lane = lax.broadcasted_iota(jnp.int32, (1, CW), 1)
    heads = [(lane // DHD == h).astype(F32) for h in range(H)]
    heads_b = [m.astype(BF16) for m in heads]
    XR = crecv.shape[1]
    key_lane = lax.broadcasted_iota(jnp.int32, (1, XR), 1)
    past = 2 * past_len
    bias_c = jnp.where((key_lane % 2 == 0) & (key_lane < past), 0.0, NEG)
    bias_o = jnp.where(lax.broadcasted_iota(jnp.int32, (1, TOK), 1) <= last, 0.0, NEG)

    o_copies = []
    for d in range(S):
        p = lax.rem(me - d + S, S)
        if d > 0:
            ca_copies[d].wait_recv()

        def attend(k, _):
            c = p * SLOTS + k
            q = qb[c]
            qs = jnp.concatenate([q * m for m in heads_b], axis=0)
            x = crecv[c]
            s = dot_nt(qs, x) + bias_c
            so = dot_nt(qs, kb[c]) + bias_o
            top = jnp.maximum(
                jnp.max(s, axis=-1, keepdims=True), jnp.max(so, axis=-1, keepdims=True)
            )
            w = jnp.exp(s - top)
            w_own = jnp.exp(so - top)
            total = jnp.sum(w, axis=-1, keepdims=True) + jnp.sum(w_own, axis=-1, keepdims=True)
            y = jnp.dot(pltpu.roll(w, 1, 1).astype(BF16), x, preferred_element_type=F32)
            y = y + jnp.dot(w_own.astype(BF16), vb[c], preferred_element_type=F32)
            y = y / total
            m = y[0:TOK] * heads[0]
            for h in range(1, H):
                m = m + y[h * TOK:(h + 1) * TOK] * heads[h]
            mx[pl.ds(pl.multiple_of(k * TOK, TOK), TOK), :] = m.astype(BF16)
            return 0

        lax.fori_loop(0, SLOTS, attend, 0, unroll=True)
        for e in range(NP):
            pt = lax.rem(p_me + e, NP)
            y = jnp.dot(
                mx[...], dout[:, pl.ds(pl.multiple_of(pt * CW, 128), CW)],
                preferred_element_type=F32,
            )
            if e == 0:
                own[d] = y
            else:
                osend[e, d] = y.astype(BF16)
                o_copies.append(
                    send(osend.at[e, d], orecv.at[e, d], o_s.at[e, d], o_r.at[e, d], at_part(e))
                )
    i = 0
    for d in range(S):
        p = lax.rem(me - d + S, S)
        mix = own[d]
        for e in range(1, NP):
            o_copies[i].wait_recv()
            mix = mix + orecv[e, d].astype(F32)
            i += 1
        mix = mix.reshape(SLOTS, TOK, CW)
        for k in range(SLOTS):
            c = p * SLOTS + k
            x = full_rows(p_me, c)
            res[c] = step_size * (x + mix[k])

    def write(qn, _):
        y = res[outidx_ref[qn]] * live_ref[qn].astype(F32)
        out_ref[qn] = y[0:last + 1, :].astype(BF16)
        return 0

    lax.fori_loop(0, SL, write, 0)
    for c in (st_copies + ca_copies[1:] + at_copies + pa_copies + g_copies + cx_copies
              + co_copies + l_copies + o_copies):
        c.wait_send()


def exclusive_rank(hot, axis):
    return jnp.sum((jnp.cumsum(hot, axis=axis) - hot) * hot, axis=-1)


def routing(complete, owner, prev_owner, S, SH, home, NS, NR):
    n = owner.shape[0]
    rng = jnp.arange(S)
    done = complete == 1
    owner_hot = ((owner[:, None] == rng[None, :]) & done[:, None]).astype(jnp.int32)
    by_home = owner_hot.reshape(S, SH, S)
    home_rank = jnp.sum(
        (jnp.cumsum(by_home, axis=1) - by_home).reshape(n, S) * owner_hot, axis=-1
    )
    prev_hot = (prev_owner[:, None] == rng[None, :]).astype(jnp.int32)
    cache_slot = exclusive_rank(prev_hot, 0)
    pair = prev_owner * S + owner
    pair_hot = ((pair[:, None] == jnp.arange(S * S)[None, :]) & done[:, None]).astype(jnp.int32)
    pair_rank = exclusive_rank(pair_hot, 0)
    ids = jnp.arange(n)
    shard = ids // SH
    local = ids - shard * SH
    slots = jnp.arange(S * SLOTS)

    def pick(valid, slot, value):
        hot = (slots[:, None] == slot[None, :]) & valid[None, :]
        return jnp.sum(jnp.where(hot, value[None, :], 0), axis=1).astype(jnp.int32), hot

    pack, _ = pick(done & (shard == home), owner * SLOTS + home_rank, local)
    cpack, _ = pick(done & (prev_owner == home), owner * SLOTS + pair_rank, cache_slot)
    crow = pack // NS * NR + pack % NS
    owned = done & (owner == home)
    home_slot = shard * SLOTS + home_rank
    cache_order = prev_owner * SLOTS + pair_rank
    order, _ = pick(owned, cache_order, home_slot)
    orow = order // SLOTS * 16 + order % SLOTS
    outidx, hot = pick(owned, home_slot, cache_order)
    live = jnp.sum(hot.astype(jnp.int32), axis=1)
    return pack, cpack, crow, order, orow, outidx, live


def shards(
    lm_query, lm_cache, language_new_pair, lm_lengths, lm_resid, lm_wo, lm_gain, lm_adapt,
    det_noise, det_pending, det_cache, det_qkv, det_out, det_gain, complete, owner, prev_owner,
):
    S, T, U = lax.axis_size("stream"), lax.axis_size("tensor"), lax.axis_size("sub")
    NP = T * U
    home = lax.axis_index("stream")
    NS = lm_query.shape[0]
    SH = NS * U
    NR = up(NS, 16)
    M = U * NR
    QW = lm_query.shape[1]
    KV = lm_cache.shape[-1] // HEAD_WIDTH
    R = QUERY_HEADS // KEY_VALUE_HEADS
    span = det_noise.shape[1]
    CW = det_noise.shape[2]
    TOK = up(span, 16)
    past = det_cache.shape[2]
    XR = up(2 * past, 128)
    SL = S * SLOTS
    CL = up(SL, 16)
    HID = lm_resid.shape[1]
    AW = lm_adapt.shape[1]

    tables = routing(complete, owner, prev_owner, S, SH, home, NS, NR)
    first = (home * U + lax.axis_index("sub")) * NS
    lengths = lax.dynamic_slice_in_dim(lm_lengths, first, NS, 0)
    LR = 2 * lm_cache.shape[1]
    lanes = jnp.arange(LR)
    bias = jnp.where(
        (lanes % 2 == 0)[None, :] & (lanes[None, :] < 2 * lengths[:, None]), 0.0, NEG
    ).astype(F32)[:, None, :]
    q = jnp.transpose(lm_query.reshape(NS, KV, R, HEAD_WIDTH), (1, 0, 2, 3))
    q = jnp.pad(q, ((0, 0), (0, 0), (0, 8 - R), (0, 0)))
    lmx = lm_cache.reshape(NS, LR, KV * HEAD_WIDTH)
    pair = jnp.transpose(
        language_new_pair.astype(F32).reshape(NS, 2, KV, HEAD_WIDTH), (1, 2, 0, 3)
    )[:, :, :, None, :]
    resid = jnp.pad(lm_resid.reshape(U, NS, HID), ((0, 0), (0, NR - NS), (0, 0))).reshape(M, HID)
    state = (
        det_noise.astype(F32) + jnp.pad(det_pending, ((0, 0), (0, 1), (0, 0))).astype(F32)
    ).astype(BF16)
    state = jnp.pad(state, ((0, 0), (0, TOK - span), (0, 0)))
    dcache = jnp.pad(
        det_cache.reshape(SH, 2 * past, CW), ((0, 0), (0, XR - 2 * past), (0, 0))
    )
    sizes = (S, T, U)
    V = pl.BlockSpec(memory_space=pltpu.VMEM)
    SM = pl.BlockSpec(memory_space=pltpu.SMEM)
    ANY = pl.BlockSpec(memory_space=pl.ANY)
    v = pltpu.VMEM
    dma = pltpu.SemaphoreType.DMA
    scratch = [
        v(lm_wo.shape, BF16), v(lm_adapt.shape, BF16), v(det_qkv.shape, BF16),
        v(det_out.shape, BF16),
        v((SL, TOK, CW), BF16), v((SL, TOK, CW), BF16),
        v((SL, XR, CW), BF16), v((SL, XR, CW), BF16),
        v((U, NR, QW), BF16), v((T, M, HID), BF16), v((U, M, AW + 128), F32),
        v((M, CW), F32), v((S * 16, CW), F32), v((S, 16, CW), BF16), v((S, 16, CW), BF16),
        v((S * 16, CW), F32), v((NP, SL, TOK, CW), BF16), v((CL, CW), F32),
        v((NP, CL, CW), BF16), v((NP, CL, CW), F32), v((SL, TOK, NP * CW), BF16),
        v((SL, TOK, CW), BF16), v((SL, TOK, CW), BF16), v((SL, TOK, CW), BF16),
        v((SLOTS * TOK, CW), BF16), v((S, SLOTS * TOK, CW), F32),
        v((NP, S, SLOTS * TOK, CW), BF16), v((NP, S, SLOTS * TOK, CW), BF16),
        v((SL, TOK, CW), F32),
        dma((4,)), dma((S,)), dma((S,)), dma((S,)), dma((S,)), dma((S,)), dma((S,)),
        dma((U,)), dma((U,)), dma((T,)), dma((T,)), dma((U,)), dma((U,)),
        dma((NP,)), dma((NP,)), dma((NP,)), dma((NP,)), dma((NP, S)), dma((NP, S)),
    ]
    hidden, new_state = pl.pallas_call(
        functools.partial(kernel, sizes, past),
        out_shape=(
            jax.ShapeDtypeStruct((M, HID), BF16),
            jax.ShapeDtypeStruct((SL, span, CW), BF16),
        ),
        in_specs=[SM] * 7 + [V] * 10 + [ANY] * 4,
        out_specs=(V, V),
        scratch_shapes=scratch,
        compiler_params=pltpu.CompilerParams(
            collective_id=0, has_side_effects=True, vmem_limit_bytes=60 * 1024 * 1024
        ),
    )(
        *tables, state, dcache, q, lmx, pair[0], pair[1], bias, resid,
        lm_gain.astype(F32)[None, :], det_gain.astype(F32)[None, :],
        lm_wo, lm_adapt, det_qkv, det_out,
    )
    hidden = hidden.reshape(U, NR, HID)[:, :NS].reshape(SH, HID)
    return hidden, new_state.reshape(1, S, SLOTS, span, CW)


def solution(mesh):
    return jax.shard_map(
        shards,
        mesh=mesh,
        in_specs=(
            P(("groups", "stream", "sub"), "tensor"),
            P(("groups", "stream", "sub"), None, None, "tensor"),
            P(("groups", "stream", "sub"), None, "tensor"),
            P("groups"),
            P(("groups", "stream"), "sub"),
            P("tensor", "sub"),
            P("sub"),
            P("sub", "tensor"),
            P(("groups", "stream"), None, ("tensor", "sub")),
            P(("groups", "stream"), None, ("tensor", "sub")),
            P(("groups", "stream"), None, None, None, ("tensor", "sub")),
            P(None, None, ("tensor", "sub")),
            P(("tensor", "sub"), None),
            P(),
            P("groups"),
            P("groups"),
            P("groups"),
        ),
        out_specs=(
            P(("groups", "stream"), "sub"),
            P(("groups", "stream"), None, None, None, ("tensor", "sub")),
        ),
        check_vma=False,
    )
```

```python
import functools

import jax
import jax.numpy as jnp
from jax import lax
from jax.experimental import pallas as pl
from jax.experimental.pallas import tpu as pltpu
from jax.sharding import PartitionSpec as P

QUERY_HEADS = 28
KEY_VALUE_HEADS = 4
HEAD_WIDTH = 128
DHD = 64
SLOTS = 6
MESH = pl.DeviceIdType.MESH

step_size = 0.5
epsilon = 1e-06
NEG = -1e30
F32 = jnp.float32
BF16 = jnp.bfloat16


def up(n, m):
    return (n + m - 1) // m * m


def dot_nt(a, b):
    return lax.dot_general(a, b, (((1,), (1,)), ((), ())), preferred_element_type=F32)


def kernel(
    sizes,
    past_len,
    tab_ref, len_ref,
    noise_ref, pend_ref, dcache_ref, query_ref, lmx_ref, pair_ref, resid_ref, gain_ref, dgain_ref,
    wo_hbm, adapt_hbm, qkv_hbm, dout_hbm,
    hid_ref, out_ref,
    wo, adapt, qkv, dout, bias_s, q_s, resid_s,
    stsend, strecv, csend, crecv, att_all, parts, condx, condf, condpack, condsend, condrecv,
    condrf, gath, n29, lg, lgf, a_s, qb, kb, vb, mx, own, osend, orecv, res,
    w_sem, st_s, st_r, ca_s, ca_r, co_s, co_r, at_s, at_r, pa_s, pa_r, cx_s, cx_r,
    g_s, g_r, l_s, l_r, o_s, o_r,
):
    S, T, U = sizes
    past = 2 * past_len
    NP = T * U
    me = lax.axis_index("stream")
    t_me = lax.axis_index("tensor")
    u_me = lax.axis_index("sub")
    p_me = t_me * U + u_me
    SL, TOK, CW = stsend.shape
    KV, NS = q_s.shape[0], q_s.shape[1]
    NR = att_all.shape[1]
    R = QUERY_HEADS // KEY_VALUE_HEADS
    last = out_ref.shape[1] - 1

    def at_stream(d):
        return {"stream": lax.rem(me + d, S)}

    def at_part(d):
        peer = lax.rem(p_me + d, NP)
        return {"tensor": lax.div(peer, U), "sub": lax.rem(peer, U)}

    def send(src, dst, ss, rs, dev):
        c = pltpu.make_async_remote_copy(
            src_ref=src, dst_ref=dst, send_sem=ss, recv_sem=rs, device_id=dev,
            device_id_type=MESH,
        )
        c.start()
        return c

    loads = []
    for i, (s, d) in enumerate(((wo_hbm, wo), (adapt_hbm, adapt), (qkv_hbm, qkv), (dout_hbm, dout))):
        c = pltpu.make_async_copy(s, d, w_sem.at[i])
        c.start()
        loads.append(c)

    barrier = pltpu.get_barrier_semaphore()
    for d in range(1, S):
        pl.semaphore_signal(barrier, inc=1, device_id=at_stream(d), device_id_type=MESH)
    for d in range(1, NP):
        pl.semaphore_signal(barrier, inc=1, device_id=at_part(d), device_id_type=MESH)

    def pack_state(i, _):
        k = tab_ref[0, i]
        pend = jnp.concatenate([pend_ref[k].astype(F32), jnp.zeros((1, CW), F32)], axis=0)
        row = noise_ref[k].astype(F32) + pend
        row = jnp.concatenate([row, jnp.zeros((TOK - last - 1, CW), F32)], axis=0)
        stsend[i] = row.astype(BF16)
        return 0

    lax.fori_loop(0, SL, pack_state, 0)
    pl.semaphore_wait(barrier, S - 1 + NP - 1)
    st_copies = []
    for d in range(1, S):
        o = lax.rem(me + d, S)
        st_copies.append(
            send(stsend.at[pl.ds(o * SLOTS, SLOTS)], strecv.at[pl.ds(me * SLOTS, SLOTS)],
                 st_s.at[d], st_r.at[d], at_stream(d))
        )

    if past < csend.shape[1]:
        csend[:, past:] = jnp.zeros((SL, csend.shape[1] - past, CW), BF16)

    def pack_cache(i, _):
        row = dcache_ref[tab_ref[1, i]].reshape(past, CW)
        csend[i, 0:past] = row
        return 0

    lax.fori_loop(0, SL, pack_cache, 0)
    ca_copies = [None]

    def send_cache(d):
        o = lax.rem(me + d, S)
        ca_copies.append(
            send(csend.at[pl.ds(o * SLOTS, SLOTS)], crecv.at[pl.ds(me * SLOTS, SLOTS)],
                 ca_s.at[d], ca_r.at[d], at_stream(d))
        )

    for d in range(1, S // 2):
        send_cache(d)

    def keep_own(i, _):
        c = me * SLOTS + i
        strecv[c] = stsend[c]
        crecv[c] = csend[c]
        return 0

    lax.fori_loop(0, SLOTS, keep_own, 0)

    scale = HEAD_WIDTH ** (-0.5)
    LR = bias_s.shape[2]
    lane_l = lax.broadcasted_iota(jnp.int32, (1, LR), 1)
    first = (me * U + u_me) * NS
    for i in range(NS):
        seen = (lane_l % 2 == 0) & (lane_l < 2 * len_ref[first + i])
        bias_s[i] = jnp.where(seen, 0.0, NEG)
    bias = bias_s[...]
    q_s[...] = jnp.zeros(q_s.shape, F32)
    for h in range(KV * R):
        q_s[h // R, :, h % R, :] = query_ref[
            :, h * HEAD_WIDTH:(h + 1) * HEAD_WIDTH
        ].astype(F32)
    if NR > NS:
        resid_s[...] = jnp.zeros(resid_s.shape, F32)
    for u in range(U):
        resid_s[u * NR:u * NR + NS] = resid_ref[...].astype(F32)[u * NS:(u + 1) * NS]
    pair = pair_ref[...].astype(F32)
    if NR > NS:
        att_all[u_me] = jnp.zeros(att_all.shape[1:], BF16)
    for kv in range(KV):
        q = q_s[kv]
        pair_kv = pair[:, :, kv * HEAD_WIDTH:(kv + 1) * HEAD_WIDTH]
        x = lmx_ref[:, :, kv * HEAD_WIDTH:(kv + 1) * HEAD_WIDTH]
        s = lax.dot_general(q.astype(BF16), x, (((2,), (2,)), ((0,), (0,))), preferred_element_type=F32)
        s = s * scale + bias
        s_new = jnp.sum(q * pair_kv[:, 0:1], axis=-1, keepdims=True) * scale
        top = jnp.maximum(jnp.max(s, axis=-1, keepdims=True), s_new)
        w = jnp.exp(s - top)
        w_new = jnp.exp(s_new - top)
        total = jnp.sum(w, axis=-1, keepdims=True) + w_new
        w_rows = w.reshape(NS * 8, w.shape[2])
        w_odd = pltpu.roll(w_rows, 1, 1).astype(BF16).reshape(w.shape)
        o = lax.dot_general(w_odd, x, (((2,), (1,)), ((0,), (0,))), preferred_element_type=F32)
        o = o + w_new.astype(BF16).astype(F32) * pair_kv[:, 1:2]
        o = o / total
        for r in range(R):
            col = (kv * R + r) * HEAD_WIDTH
            att_all[u_me, 0:NS, col:col + HEAD_WIDTH] = o[:, r, :].astype(BF16)
    at_copies = []
    for d in range(1, U):
        at_copies.append(
            send(att_all.at[u_me], att_all.at[u_me], at_s.at[d], at_r.at[d],
                 {"sub": lax.rem(u_me + d, U)})
        )
    for c in at_copies:
        c.wait_recv()
    loads[0].wait()
    M = U * NR
    att = att_all[...].reshape(M, att_all.shape[2])
    parts[t_me] = jnp.dot(att, wo[...], preferred_element_type=F32).astype(BF16)
    pa_copies = []
    for d in range(1, T):
        pa_copies.append(
            send(parts.at[t_me], parts.at[t_me], pa_s.at[d], pa_r.at[d],
                 {"tensor": lax.rem(t_me + d, T)})
        )
    for c in st_copies:
        c.wait_recv()

    def arrange(c, _):
        row = strecv[tab_ref[3, c]]
        gath[p_me, c] = row
        n29[pl.ds(c, 1), :] = row.astype(F32)[last:last + 1, :]
        return 0

    lax.fori_loop(0, SL, arrange, 0)
    for c in pa_copies:
        c.wait_recv()
    g_copies = []
    for d in range(1, NP):
        g_copies.append(send(gath.at[p_me], gath.at[p_me], g_s.at[d], g_r.at[d], at_part(d)))
    mixing = parts[0].astype(F32)
    for t in range(1, T):
        mixing = mixing + parts[t].astype(F32)
    hidden = (resid_s[...] + mixing).astype(BF16)
    for u in range(U):
        hid_ref[u * NS:(u + 1) * NS] = hidden[u * NR:u * NR + NS]
    wide = hidden.astype(F32)
    gained = (wide * gain_ref[...].astype(F32)).astype(BF16)
    loads[1].wait()
    AW = adapt.shape[1]
    condx[u_me, :, 0:AW] = jnp.dot(gained, adapt[...], preferred_element_type=F32)
    condx[u_me, :, AW:AW + 128] = jnp.broadcast_to(
        jnp.sum(wide * wide, axis=-1, keepdims=True), (M, 128)
    )
    cx_copies = []
    for d in range(1, U):
        cx_copies.append(
            send(condx.at[u_me], condx.at[u_me], cx_s.at[d], cx_r.at[d],
                 {"sub": lax.rem(u_me + d, U)})
        )
    condpack[...] = jnp.zeros(condpack.shape, F32)
    for c in cx_copies:
        c.wait_recv()
    mine = pl.ds(pl.multiple_of(u_me * CW, 128), CW)
    acc, sq = condx[0, :, mine], condx[0, :, AW:AW + 128]
    for u in range(1, U):
        acc = acc + condx[u, :, mine]
        sq = sq + condx[u, :, AW:AW + 128]
    inv = lax.rsqrt(sq[:, 0:1] / (hidden.shape[1] * U) + epsilon)
    condf[...] = acc * inv

    def pack_cond(o, _):
        for r in range(SLOTS):
            condpack[pl.ds(o * 16 + r, 1), :] = condf[pl.ds(tab_ref[2, o * SLOTS + r], 1), :]
        return 0

    lax.fori_loop(0, S, pack_cond, 0)
    condsend[...] = condpack[...].astype(BF16).reshape(condsend.shape)
    co_copies = []
    for d in range(1, S):
        o = lax.rem(me + d, S)
        co_copies.append(
            send(condsend.at[o], condrecv.at[me], co_s.at[d], co_r.at[d], at_stream(d))
        )
    for d in range(max(1, S // 2), S):
        send_cache(d)
    condrecv[me] = condsend[me]
    lgf[...] = jnp.zeros(lgf.shape, F32)
    for c in co_copies:
        c.wait_recv()
    condrf[...] = condrecv[...].astype(F32).reshape(condrf.shape)

    def last_rows(c, _):
        lgf[p_me, pl.ds(c, 1), :] = n29[pl.ds(c, 1), :] + condrf[pl.ds(tab_ref[4, c], 1), :]
        return 0

    lax.fori_loop(0, SL, last_rows, 0)
    lg[p_me] = lgf[p_me].astype(BF16)
    l_copies = []
    for d in range(1, NP):
        l_copies.append(send(lg.at[p_me], lg.at[p_me], l_s.at[d], l_r.at[d], at_part(d)))
    for c in g_copies:
        c.wait_recv()
    for c in l_copies:
        c.wait_recv()
    lgf[...] = lg[...].astype(F32)

    is_last = lax.broadcasted_iota(jnp.int32, (TOK, CW), 0) == last

    def full_rows(part, c):
        return jnp.where(is_last, lgf[part, pl.ds(c, 1), :], gath[part, c].astype(F32))

    dgain = dgain_ref[...].astype(F32)

    def normalize(c, _):
        rows = [full_rows(pt, c) for pt in range(NP)]
        ss = rows[0] * rows[0]
        for x in rows[1:]:
            ss = ss + x * x
        inv = lax.rsqrt(jnp.sum(ss, axis=-1, keepdims=True) / (NP * CW) + epsilon)
        for pt in range(NP):
            a_s[c, :, pt * CW:(pt + 1) * CW] = (
                rows[pt] * inv * dgain[:, pt * CW:(pt + 1) * CW]
            ).astype(BF16)
        return 0

    lax.fori_loop(0, SL, normalize, 0)
    loads[2].wait()
    loads[3].wait()

    def project(p, _):
        here = pl.ds(p * SLOTS, SLOTS)
        a = a_s[here].reshape(SLOTS * TOK, NP * CW)
        for k, dst in enumerate((qb, kb, vb)):
            y = jnp.dot(a, qkv[k], preferred_element_type=F32)
            if k == 0:
                y = y * (DHD ** (-0.5))
            dst[here] = y.astype(BF16).reshape(SLOTS, TOK, CW)
        return 0

    lax.fori_loop(0, S, project, 0)

    H = CW // DHD
    lane = lax.broadcasted_iota(jnp.int32, (1, CW), 1)
    heads = [(lane // DHD == h).astype(F32) for h in range(H)]
    heads_b = [m.astype(BF16) for m in heads]
    XR = crecv.shape[1]
    key_lane = lax.broadcasted_iota(jnp.int32, (1, XR), 1)
    bias_c = jnp.where((key_lane % 2 == 0) & (key_lane < past), 0.0, NEG)
    bias_o = jnp.where(lax.broadcasted_iota(jnp.int32, (1, TOK), 1) <= last, 0.0, NEG)

    o_copies = []
    for d in range(S):
        p = lax.rem(me - d + S, S)
        if d > 0:
            ca_copies[d].wait_recv()

        def attend(k, _):
            c = p * SLOTS + k
            q = qb[c]
            qs = jnp.concatenate([q * m for m in heads_b], axis=0)
            x = crecv[c]
            s = dot_nt(qs, x) + bias_c
            so = dot_nt(qs, kb[c]) + bias_o
            top = jnp.maximum(
                jnp.max(s, axis=-1, keepdims=True), jnp.max(so, axis=-1, keepdims=True)
            )
            w = jnp.exp(s - top)
            w_own = jnp.exp(so - top)
            total = jnp.sum(w, axis=-1, keepdims=True) + jnp.sum(w_own, axis=-1, keepdims=True)
            y = jnp.dot(pltpu.roll(w, 1, 1).astype(BF16), x, preferred_element_type=F32)
            y = y + jnp.dot(w_own.astype(BF16), vb[c], preferred_element_type=F32)
            y = y / total
            m = y[0:TOK] * heads[0]
            for h in range(1, H):
                m = m + y[h * TOK:(h + 1) * TOK] * heads[h]
            mx[pl.ds(pl.multiple_of(k * TOK, TOK), TOK), :] = m.astype(BF16)
            return 0

        lax.fori_loop(0, SLOTS, attend, 0, unroll=True)
        for e in range(NP):
            pt = lax.rem(p_me + e, NP)
            y = jnp.dot(
                mx[...], dout[:, pl.ds(pl.multiple_of(pt * CW, 128), CW)],
                preferred_element_type=F32,
            )
            if e == 0:
                own[d] = y
            else:
                osend[e, d] = y.astype(BF16)
                o_copies.append(
                    send(osend.at[e, d], orecv.at[e, d], o_s.at[e, d], o_r.at[e, d], at_part(e))
                )
    i = 0
    for d in range(S):
        p = lax.rem(me - d + S, S)
        mix = own[d]
        for e in range(1, NP):
            o_copies[i].wait_recv()
            mix = mix + orecv[e, d].astype(F32)
            i += 1
        mix = mix.reshape(SLOTS, TOK, CW)
        for k in range(SLOTS):
            c = p * SLOTS + k
            x = full_rows(p_me, c)
            res[c] = step_size * (x + mix[k])

    def write(qn, _):
        y = res[tab_ref[5, qn]] * tab_ref[6, qn].astype(F32)
        out_ref[qn] = y[0:last + 1, :].astype(BF16)
        return 0

    lax.fori_loop(0, SL, write, 0)
    for c in (st_copies + ca_copies[1:] + at_copies + pa_copies + g_copies + cx_copies
              + co_copies + l_copies + o_copies):
        c.wait_send()


def routing_kernel(dims, done_ref, owner_ref, prev_ref, tab_ref):
    S, SH, NS, NR = dims
    n = done_ref.shape[1]
    home = lax.axis_index("stream")
    done = done_ref[...] == 1
    owner = owner_ref[...]
    prev = prev_ref[...]
    before = lax.broadcasted_iota(jnp.int32, (n, n), 0)
    after = lax.broadcasted_iota(jnp.int32, (n, n), 1)
    earlier = (before < after).astype(F32)
    same = jnp.where(before // SH == after // SH, earlier, 0.0).astype(BF16)
    earlier = earlier.astype(BF16)

    def rank(key, count, valid, order):
        rows = lax.broadcasted_iota(jnp.int32, (count, n), 0)
        hot = jnp.where((rows == key) & valid, 1.0, 0.0)
        cum = jnp.dot(hot.astype(BF16), order, preferred_element_type=F32)
        return jnp.sum(cum * hot, axis=0, keepdims=True)

    always = owner >= 0
    home_rank = rank(owner, S, done, same)
    cache_slot = rank(prev, S, always, earlier)
    pair_rank = rank(prev * S + owner, S * S, done, earlier).astype(jnp.int32)
    ids = lax.broadcasted_iota(jnp.int32, (1, n), 1)
    shard = ids // SH
    local = (ids - shard * SH).astype(F32)
    home_slot = shard * SLOTS + home_rank.astype(jnp.int32)
    target = owner * SLOTS + home_rank.astype(jnp.int32)
    cache_order = prev * SLOTS + pair_rank
    width = tab_ref.shape[1]
    slots = lax.broadcasted_iota(jnp.int32, (width, n), 0)

    def pick(valid, slot, value):
        hot = jnp.where((slots == slot) & valid, 1.0, 0.0).astype(BF16)
        value = jnp.broadcast_to(value, (8, n)).astype(BF16)
        return dot_nt(value, hot)[0:1].astype(jnp.int32)

    pack = pick(done & (shard == home), target, local)
    owned = done & (owner == home)
    order = pick(owned, cache_order, home_slot.astype(F32))
    tab_ref[0:1] = pack
    tab_ref[1:2] = pick(done & (prev == home), owner * SLOTS + pair_rank, cache_slot)
    tab_ref[2:3] = pack // NS * NR + pack % NS
    tab_ref[3:4] = order
    tab_ref[4:5] = order // SLOTS * 16 + order % SLOTS
    tab_ref[5:6] = pick(owned, home_slot, cache_order.astype(F32))
    tab_ref[6:7] = pick(owned, home_slot, jnp.ones((1, n), F32))
    tab_ref[7:8] = jnp.zeros((1, width), jnp.int32)


def shards(
    lm_query, lm_cache, language_new_pair, lm_lengths, lm_resid, lm_wo, lm_gain, lm_adapt,
    det_noise, det_pending, det_cache, det_qkv, det_out, det_gain, complete, owner, prev_owner,
):
    S, T, U = lax.axis_size("stream"), lax.axis_size("tensor"), lax.axis_size("sub")
    NP = T * U
    home = lax.axis_index("stream")
    NS = lm_query.shape[0]
    SH = NS * U
    NR = up(NS, 16)
    M = U * NR
    QW = lm_query.shape[1]
    KV = lm_cache.shape[-1] // HEAD_WIDTH
    R = QUERY_HEADS // KEY_VALUE_HEADS
    span = det_noise.shape[1]
    CW = det_noise.shape[2]
    TOK = up(span, 16)
    past = det_cache.shape[2]
    XR = up(2 * past, 128)
    SL = S * SLOTS
    CL = up(SL, 16)
    HID = lm_resid.shape[1]
    AW = lm_adapt.shape[1]

    n = owner.shape[0]
    tables = pl.pallas_call(
        functools.partial(routing_kernel, (S, SH, NS, NR)),
        out_shape=jax.ShapeDtypeStruct((8, up(SL, 128)), jnp.int32),
        compiler_params=pltpu.CompilerParams(vmem_limit_bytes=60 * 1024 * 1024),
    )(complete.reshape(1, n), owner.reshape(1, n), prev_owner.reshape(1, n))
    LR = 2 * lm_cache.shape[1]
    lmx = lm_cache.reshape(NS, LR, KV * HEAD_WIDTH)
    dcache = det_cache.reshape(SH, past, 2, CW)
    sizes = (S, T, U)
    V = pl.BlockSpec(memory_space=pltpu.VMEM)
    SM = pl.BlockSpec(memory_space=pltpu.SMEM)
    ANY = pl.BlockSpec(memory_space=pl.ANY)
    v = pltpu.VMEM
    dma = pltpu.SemaphoreType.DMA
    scratch = [
        v(lm_wo.shape, BF16), v(lm_adapt.shape, BF16), v(det_qkv.shape, BF16),
        v(det_out.shape, BF16), v((NS, 1, LR), F32), v((KV, NS, 8, HEAD_WIDTH), F32),
        v((M, HID), F32),
        v((SL, TOK, CW), BF16), v((SL, TOK, CW), BF16),
        v((SL, XR, CW), BF16), v((SL, XR, CW), BF16),
        v((U, NR, QW), BF16), v((T, M, HID), BF16), v((U, M, AW + 128), F32),
        v((M, CW), F32), v((S * 16, CW), F32), v((S, 16, CW), BF16), v((S, 16, CW), BF16),
        v((S * 16, CW), F32), v((NP, SL, TOK, CW), BF16), v((CL, CW), F32),
        v((NP, CL, CW), BF16), v((NP, CL, CW), F32), v((SL, TOK, NP * CW), BF16),
        v((SL, TOK, CW), BF16), v((SL, TOK, CW), BF16), v((SL, TOK, CW), BF16),
        v((SLOTS * TOK, CW), BF16), v((S, SLOTS * TOK, CW), F32),
        v((NP, S, SLOTS * TOK, CW), BF16), v((NP, S, SLOTS * TOK, CW), BF16),
        v((SL, TOK, CW), F32),
        dma((4,)), dma((S,)), dma((S,)), dma((S,)), dma((S,)), dma((S,)), dma((S,)),
        dma((U,)), dma((U,)), dma((T,)), dma((T,)), dma((U,)), dma((U,)),
        dma((NP,)), dma((NP,)), dma((NP,)), dma((NP,)), dma((NP, S)), dma((NP, S)),
    ]
    hidden, new_state = pl.pallas_call(
        functools.partial(kernel, sizes, past),
        out_shape=(
            jax.ShapeDtypeStruct((SH, HID), BF16),
            jax.ShapeDtypeStruct((SL, span, CW), BF16),
        ),
        in_specs=[SM] * 2 + [V] * 9 + [ANY] * 4,
        out_specs=(V, V),
        scratch_shapes=scratch,
        compiler_params=pltpu.CompilerParams(
            collective_id=0, has_side_effects=True, vmem_limit_bytes=60 * 1024 * 1024
        ),
    )(
        tables, lm_lengths, det_noise, det_pending, dcache, lm_query, lmx, language_new_pair,
        lm_resid, lm_gain[None, :], det_gain[None, :],
        lm_wo, lm_adapt, det_qkv, det_out,
    )
    return hidden, new_state.reshape(1, S, SLOTS, span, CW)


def solution(mesh):
    return jax.shard_map(
        shards,
        mesh=mesh,
        in_specs=(
            P(("groups", "stream", "sub"), "tensor"),
            P(("groups", "stream", "sub"), None, None, "tensor"),
            P(("groups", "stream", "sub"), None, "tensor"),
            P("groups"),
            P(("groups", "stream"), "sub"),
            P("tensor", "sub"),
            P("sub"),
            P("sub", "tensor"),
            P(("groups", "stream"), None, ("tensor", "sub")),
            P(("groups", "stream"), None, ("tensor", "sub")),
            P(("groups", "stream"), None, None, None, ("tensor", "sub")),
            P(None, None, ("tensor", "sub")),
            P(("tensor", "sub"), None),
            P(),
            P("groups"),
            P("groups"),
            P("groups"),
        ),
        out_specs=(
            P(("groups", "stream"), "sub"),
            P(("groups", "stream"), None, None, None, ("tensor", "sub")),
        ),
        check_vma=False,
    )
```

```python
import functools

import jax
import jax.numpy as jnp
from jax import lax
from jax.experimental import pallas as pl
from jax.experimental.pallas import tpu as pltpu
from jax.sharding import PartitionSpec as P

QUERY_HEADS = 28
KEY_VALUE_HEADS = 4
HEAD_WIDTH = 128
DHD = 64
SLOTS = 6
MESH = pl.DeviceIdType.MESH

step_size = 0.5
epsilon = 1e-06
NEG = -1e30
F32 = jnp.float32
BF16 = jnp.bfloat16


def up(n, m):
    return (n + m - 1) // m * m


def dot_nt(a, b):
    return lax.dot_general(a, b, (((1,), (1,)), ((), ())), preferred_element_type=F32)


def kernel(
    sizes,
    past_len,
    tab_ref, len_ref,
    noise_ref, pend_ref, dcache_ref, query_ref, lmx_ref, pair_ref, resid_ref, gain_ref, dgain_ref,
    wo_hbm, adapt_hbm, qkv_hbm, dout_hbm,
    hid_ref, out_ref,
    wo, adapt, qkv, dout, bias_s, q_s, resid_s,
    stsend, strecv, csend, crecv, att_all, parts, condx, condf, condpack, condsend, condrecv,
    condrf, gath, n29, lg, lgf, a_s, qb, kb, vb, mx, own, ocs, ocr, oxs, oxr, res,
    w_sem, st_s, st_r, ca_s, ca_r, co_s, co_r, at_s, at_r, pa_s, pa_r, cx_s, cx_r,
    g_s, g_r, gc_s, gc_r, l_s, l_r, oc_s, oc_r, o_s, o_r,
):
    S, T, U = sizes
    past = 2 * past_len
    NP = T * U
    me = lax.axis_index("stream")
    t_me = lax.axis_index("tensor")
    u_me = lax.axis_index("sub")
    p_me = t_me * U + u_me
    SL, TOK, CW = stsend.shape
    KV, NS = q_s.shape[0], q_s.shape[1]
    NR = att_all.shape[1]
    R = QUERY_HEADS // KEY_VALUE_HEADS
    last = out_ref.shape[1] - 1

    def row_of(ref):
        g = ref[...].astype(F32)
        return jnp.concatenate([g[i:i + 1] for i in range(g.shape[0])], axis=1)

    def at_stream(d):
        return {"stream": lax.rem(me + d, S)}

    def at_part(d):
        peer = lax.rem(p_me + d, NP)
        return {"tensor": lax.div(peer, U), "sub": lax.rem(peer, U)}

    def send(src, dst, ss, rs, dev):
        c = pltpu.make_async_remote_copy(
            src_ref=src, dst_ref=dst, send_sem=ss, recv_sem=rs, device_id=dev,
            device_id_type=MESH,
        )
        c.start()
        return c

    loads = []
    for i, (s, d) in enumerate(((wo_hbm, wo), (adapt_hbm, adapt), (qkv_hbm, qkv), (dout_hbm, dout))):
        c = pltpu.make_async_copy(s, d, w_sem.at[i])
        c.start()
        loads.append(c)

    barrier = pltpu.get_barrier_semaphore()
    for d in range(1, S):
        pl.semaphore_signal(barrier, inc=1, device_id=at_stream(d), device_id_type=MESH)
    for d in range(1, NP):
        pl.semaphore_signal(barrier, inc=1, device_id=at_part(d), device_id_type=MESH)

    def pack_state(i, _):
        k = tab_ref[0, i]
        pend = jnp.concatenate([pend_ref[k].astype(F32), jnp.zeros((1, CW), F32)], axis=0)
        row = noise_ref[k].astype(F32) + pend
        row = jnp.concatenate([row, jnp.zeros((TOK - last - 1, CW), F32)], axis=0)
        stsend[i] = row.astype(BF16)
        return 0

    lax.fori_loop(0, SL, pack_state, 0)
    pl.semaphore_wait(barrier, S - 1 + NP - 1)
    st_copies = []
    for d in range(1, S):
        o = lax.rem(me + d, S)
        st_copies.append(
            send(stsend.at[pl.ds(o * SLOTS, SLOTS)], strecv.at[pl.ds(me * SLOTS, SLOTS)],
                 st_s.at[d], st_r.at[d], at_stream(d))
        )

    if past < csend.shape[1]:
        csend[:, past:] = jnp.zeros((SL, csend.shape[1] - past, CW), BF16)

    def pack_cache(i, _):
        row = dcache_ref[tab_ref[1, i]].reshape(past, CW)
        csend[i, 0:past] = row
        return 0

    def pack_block(d):
        o = lax.rem(me + d, S)
        lax.fori_loop(o * SLOTS, o * SLOTS + SLOTS, pack_cache, 0)

    ca_copies = [None]

    def send_cache(d):
        o = lax.rem(me + d, S)
        ca_copies.append(
            send(csend.at[pl.ds(o * SLOTS, SLOTS)], crecv.at[pl.ds(me * SLOTS, SLOTS)],
                 ca_s.at[d], ca_r.at[d], at_stream(d))
        )

    for d in range(1, S // 2):
        pack_block(d)
        send_cache(d)

    def keep_own(i, _):
        c = me * SLOTS + i
        strecv[c] = stsend[c]
        crecv[c] = csend[c]
        return 0


    scale = HEAD_WIDTH ** (-0.5)
    LR = bias_s.shape[2]
    lane_l = lax.broadcasted_iota(jnp.int32, (1, LR), 1)
    first = (me * U + u_me) * NS
    for i in range(NS):
        seen = (lane_l % 2 == 0) & (lane_l < 2 * len_ref[first + i])
        bias_s[i] = jnp.where(seen, 0.0, NEG)
    bias = bias_s[...]
    q_s[...] = jnp.zeros(q_s.shape, F32)
    for h in range(KV * R):
        q_s[h // R, :, h % R, :] = query_ref[
            :, h * HEAD_WIDTH:(h + 1) * HEAD_WIDTH
        ].astype(F32)
    if NR > NS:
        resid_s[...] = jnp.zeros(resid_s.shape, F32)
    for u in range(U):
        resid_s[u * NR:u * NR + NS] = resid_ref[...].astype(F32)[u * NS:(u + 1) * NS]
    pair = pair_ref[...].astype(F32)
    if NR > NS:
        att_all[u_me] = jnp.zeros(att_all.shape[1:], BF16)
    for kv in range(KV):
        q = q_s[kv]
        pair_kv = pair[:, :, kv * HEAD_WIDTH:(kv + 1) * HEAD_WIDTH]
        x = lmx_ref[:, :, :, kv * HEAD_WIDTH:(kv + 1) * HEAD_WIDTH].reshape(NS, LR, HEAD_WIDTH)
        s = lax.dot_general(q.astype(BF16), x, (((2,), (2,)), ((0,), (0,))), preferred_element_type=F32)
        s = s * scale + bias
        s_new = jnp.sum(q * pair_kv[:, 0:1], axis=-1, keepdims=True) * scale
        top = jnp.maximum(jnp.max(s, axis=-1, keepdims=True), s_new)
        w = jnp.exp(s - top)
        w_new = jnp.exp(s_new - top)
        total = jnp.sum(w, axis=-1, keepdims=True) + w_new
        w_rows = w.reshape(NS * 8, w.shape[2])
        w_odd = pltpu.roll(w_rows, 1, 1).astype(BF16).reshape(w.shape)
        o = lax.dot_general(w_odd, x, (((2,), (1,)), ((0,), (0,))), preferred_element_type=F32)
        o = o + w_new.astype(BF16).astype(F32) * pair_kv[:, 1:2]
        o = o / total
        for r in range(R):
            col = (kv * R + r) * HEAD_WIDTH
            att_all[u_me, 0:NS, col:col + HEAD_WIDTH] = o[:, r, :].astype(BF16)
    at_copies = []
    for d in range(1, U):
        at_copies.append(
            send(att_all.at[u_me], att_all.at[u_me], at_s.at[d], at_r.at[d],
                 {"sub": lax.rem(u_me + d, U)})
        )
    late = list(range(max(1, S // 2), S))
    pack_block(0)
    lax.fori_loop(0, SLOTS, keep_own, 0)
    for d in late[:len(late) // 2]:
        pack_block(d)
    for c in at_copies:
        c.wait_recv()
    loads[0].wait()
    M = U * NR
    att = att_all[...].reshape(M, att_all.shape[2])
    parts[t_me] = jnp.dot(att, wo[...], preferred_element_type=F32).astype(BF16)
    pa_copies = []
    for d in range(1, T):
        pa_copies.append(
            send(parts.at[t_me], parts.at[t_me], pa_s.at[d], pa_r.at[d],
                 {"tensor": lax.rem(t_me + d, T)})
        )
    for d in late[len(late) // 2:]:
        pack_block(d)
    for c in st_copies:
        c.wait_recv()

    def arrange(c, _):
        row = strecv[tab_ref[3, c]]
        gath[p_me, c] = row
        n29[pl.ds(c, 1), :] = row.astype(F32)[last:last + 1, :]
        return 0

    lax.fori_loop(0, SL, arrange, 0)
    for c in pa_copies:
        c.wait_recv()
    g_copies, gc_copies = [], []

    def share(j, part):
        for e in range(1, U):
            i = (e - 1) * T + j
            gc_copies.append(
                send(gath.at[part], gath.at[part], gc_s.at[i], gc_r.at[i],
                     {"sub": lax.rem(u_me + e, U)})
            )

    for d in range(1, T):
        g_copies.append(
            send(gath.at[p_me], gath.at[p_me], g_s.at[d], g_r.at[d],
                 {"tensor": lax.rem(t_me + d, T)})
        )
    share(0, p_me)
    mixing = parts[0].astype(F32)
    for t in range(1, T):
        mixing = mixing + parts[t].astype(F32)
    hidden = (resid_s[...] + mixing).astype(BF16)
    for u in range(U):
        hid_ref[u * NS:(u + 1) * NS] = hidden[u * NR:u * NR + NS]
    wide = hidden.astype(F32)
    gained = (wide * row_of(gain_ref)).astype(BF16)
    loads[1].wait()
    AW = adapt.shape[1]
    condx[u_me, :, 0:AW] = jnp.dot(gained, adapt[...], preferred_element_type=F32)
    condx[u_me, :, AW:AW + 128] = jnp.broadcast_to(
        jnp.sum(wide * wide, axis=-1, keepdims=True), (M, 128)
    )
    cx_copies = []
    for d in range(1, U):
        cx_copies.append(
            send(condx.at[u_me], condx.at[u_me], cx_s.at[d], cx_r.at[d],
                 {"sub": lax.rem(u_me + d, U)})
        )
    condpack[...] = jnp.zeros(condpack.shape, F32)
    for c in cx_copies:
        c.wait_recv()
    mine = pl.ds(pl.multiple_of(u_me * CW, 128), CW)
    acc, sq = condx[0, :, mine], condx[0, :, AW:AW + 128]
    for u in range(1, U):
        acc = acc + condx[u, :, mine]
        sq = sq + condx[u, :, AW:AW + 128]
    inv = lax.rsqrt(sq[:, 0:1] / (hidden.shape[1] * U) + epsilon)
    condf[...] = acc * inv

    def pack_cond(o, _):
        for r in range(SLOTS):
            condpack[pl.ds(o * 16 + r, 1), :] = condf[pl.ds(tab_ref[2, o * SLOTS + r], 1), :]
        return 0

    lax.fori_loop(0, S, pack_cond, 0)
    condsend[...] = condpack[...].astype(BF16).reshape(condsend.shape)
    co_copies = []
    for d in range(1, S):
        o = lax.rem(me + d, S)
        co_copies.append(
            send(condsend.at[o], condrecv.at[me], co_s.at[d], co_r.at[d], at_stream(d))
        )
    for d in late:
        send_cache(d)
    condrecv[me] = condsend[me]
    lgf[...] = jnp.zeros(lgf.shape, F32)
    for d in range(1, T):
        g_copies[d - 1].wait_recv()
        share(d, lax.rem(t_me - d + T, T) * U + u_me)
    for c in co_copies:
        c.wait_recv()
    condrf[...] = condrecv[...].astype(F32).reshape(condrf.shape)

    def last_rows(c, _):
        lgf[p_me, pl.ds(c, 1), :] = n29[pl.ds(c, 1), :] + condrf[pl.ds(tab_ref[4, c], 1), :]
        return 0

    lax.fori_loop(0, SL, last_rows, 0)
    lg[p_me] = lgf[p_me].astype(BF16)
    l_copies = []
    for d in range(1, NP):
        l_copies.append(send(lg.at[p_me], lg.at[p_me], l_s.at[d], l_r.at[d], at_part(d)))
    for c in gc_copies:
        c.wait_recv()
    for c in l_copies:
        c.wait_recv()
    lgf[...] = lg[...].astype(F32)

    is_last = lax.broadcasted_iota(jnp.int32, (TOK, CW), 0) == last

    def full_rows(part, c):
        return jnp.where(is_last, lgf[part, pl.ds(c, 1), :], gath[part, c].astype(F32))

    dgain = row_of(dgain_ref)

    def normalize(c, _):
        rows = [full_rows(pt, c) for pt in range(NP)]
        ss = rows[0] * rows[0]
        for x in rows[1:]:
            ss = ss + x * x
        inv = lax.rsqrt(jnp.sum(ss, axis=-1, keepdims=True) / (NP * CW) + epsilon)
        for pt in range(NP):
            a_s[c, :, pt * CW:(pt + 1) * CW] = (
                rows[pt] * inv * dgain[:, pt * CW:(pt + 1) * CW]
            ).astype(BF16)
        return 0

    lax.fori_loop(0, SL, normalize, 0)
    loads[2].wait()
    loads[3].wait()

    def project(p, _):
        here = pl.ds(p * SLOTS, SLOTS)
        a = a_s[here].reshape(SLOTS * TOK, NP * CW)
        for k, dst in enumerate((qb, kb, vb)):
            y = jnp.dot(a, qkv[k], preferred_element_type=F32)
            if k == 0:
                y = y * (DHD ** (-0.5))
            dst[here] = y.astype(BF16).reshape(SLOTS, TOK, CW)
        return 0

    lax.fori_loop(0, S, project, 0)

    H = CW // DHD
    lane = lax.broadcasted_iota(jnp.int32, (1, CW), 1)
    heads = [(lane // DHD == h).astype(F32) for h in range(H)]
    heads_b = [m.astype(BF16) for m in heads]
    XR = crecv.shape[1]
    key_lane = lax.broadcasted_iota(jnp.int32, (1, XR), 1)
    bias_c = jnp.where((key_lane % 2 == 0) & (key_lane < past), 0.0, NEG)
    bias_o = jnp.where(lax.broadcasted_iota(jnp.int32, (1, TOK), 1) <= last, 0.0, NEG)

    o_copies = [[] for _ in range(S)]
    oc_copies = [[] for _ in range(S)]

    def across(d):
        for c in oc_copies[d]:
            c.wait_recv()
        for j in list(range(1, T)) + [0]:
            y = own[d, j]
            for e in range(1, U):
                y = y + ocr[e - 1, d, j].astype(F32)
            if j == 0:
                own[d, j] = y
            else:
                oxs[j - 1, d] = y.astype(BF16)
                o_copies[d].append(
                    send(oxs.at[j - 1, d], oxr.at[j - 1, d], o_s.at[j, d], o_r.at[j, d],
                         {"tensor": lax.rem(t_me + j, T)})
                )

    for d in range(S):
        p = lax.rem(me - d + S, S)
        if d > 0:
            ca_copies[d].wait_recv()

        def attend(k, _):
            c = p * SLOTS + k
            q = qb[c]
            qs = jnp.concatenate([q * m for m in heads_b], axis=0)
            x = crecv[c]
            s = dot_nt(qs, x) + bias_c
            so = dot_nt(qs, kb[c]) + bias_o
            top = jnp.maximum(
                jnp.max(s, axis=-1, keepdims=True), jnp.max(so, axis=-1, keepdims=True)
            )
            w = jnp.exp(s - top)
            w_own = jnp.exp(so - top)
            total = jnp.sum(w, axis=-1, keepdims=True) + jnp.sum(w_own, axis=-1, keepdims=True)
            y = jnp.dot(pltpu.roll(w, 1, 1).astype(BF16), x, preferred_element_type=F32)
            y = y + jnp.dot(w_own.astype(BF16), vb[c], preferred_element_type=F32)
            y = y / total
            m = y[0:TOK] * heads[0]
            for h in range(1, H):
                m = m + y[h * TOK:(h + 1) * TOK] * heads[h]
            mx[pl.ds(pl.multiple_of(k * TOK, TOK), TOK), :] = m.astype(BF16)
            return 0

        lax.fori_loop(0, SLOTS, attend, 0, unroll=True)
        for e in range(U):
            u = lax.rem(u_me + e, U)
            for j in range(T):
                pt = lax.rem(t_me + j, T) * U + u
                y = jnp.dot(
                    mx[...], dout[:, pl.ds(pl.multiple_of(pt * CW, 128), CW)],
                    preferred_element_type=F32,
                )
                if e == 0:
                    own[d, j] = y
                else:
                    ocs[e - 1, d, j] = y.astype(BF16)
            if e > 0:
                oc_copies[d].append(
                    send(ocs.at[e - 1, d], ocr.at[e - 1, d], oc_s.at[e, d], oc_r.at[e, d], {"sub": u})
                )
        if d > 0:
            across(d - 1)
    across(S - 1)
    for d in range(S):
        p = lax.rem(me - d + S, S)
        mix = own[d, 0]
        for j in range(1, T):
            o_copies[d][j - 1].wait_recv()
            mix = mix + oxr[j - 1, d].astype(F32)
        mix = mix.reshape(SLOTS, TOK, CW)
        for k in range(SLOTS):
            c = p * SLOTS + k
            x = full_rows(p_me, c)
            res[c] = step_size * (x + mix[k])

    def write(qn, _):
        y = res[tab_ref[5, qn]] * tab_ref[6, qn].astype(F32)
        out_ref[qn] = y[0:last + 1, :].astype(BF16)
        return 0

    lax.fori_loop(0, SL, write, 0)
    for c in (sum(o_copies, []) + sum(oc_copies, []) + gc_copies + st_copies + ca_copies[1:] + at_copies + pa_copies + g_copies + cx_copies
              + co_copies + l_copies):
        c.wait_send()


def routing_kernel(dims, done_ref, owner_ref, prev_ref, tab_ref):
    S, SH, NS, NR = dims
    n = done_ref.shape[1]
    home = lax.axis_index("stream")
    done = done_ref[...] == 1
    owner = owner_ref[...]
    prev = prev_ref[...]
    before = lax.broadcasted_iota(jnp.int32, (n, n), 0)
    after = lax.broadcasted_iota(jnp.int32, (n, n), 1)
    earlier = (before < after).astype(F32)
    same = jnp.where(before // SH == after // SH, earlier, 0.0).astype(BF16)
    earlier = earlier.astype(BF16)

    def rank(key, count, valid, order):
        rows = lax.broadcasted_iota(jnp.int32, (count, n), 0)
        hot = jnp.where((rows == key) & valid, 1.0, 0.0)
        cum = jnp.dot(hot.astype(BF16), order, preferred_element_type=F32)
        return jnp.sum(cum * hot, axis=0, keepdims=True)

    always = owner >= 0
    home_rank = rank(owner, S, done, same)
    cache_slot = rank(prev, S, always, earlier)
    pair_rank = rank(prev * S + owner, S * S, done, earlier).astype(jnp.int32)
    ids = lax.broadcasted_iota(jnp.int32, (1, n), 1)
    shard = ids // SH
    local = (ids - shard * SH).astype(F32)
    home_slot = shard * SLOTS + home_rank.astype(jnp.int32)
    target = owner * SLOTS + home_rank.astype(jnp.int32)
    cache_order = prev * SLOTS + pair_rank
    width = tab_ref.shape[1]
    slots = lax.broadcasted_iota(jnp.int32, (width, n), 0)

    def pick(valid, slot, value):
        hot = jnp.where((slots == slot) & valid, 1.0, 0.0).astype(BF16)
        value = jnp.broadcast_to(value, (8, n)).astype(BF16)
        return dot_nt(value, hot)[0:1].astype(jnp.int32)

    pack = pick(done & (shard == home), target, local)
    owned = done & (owner == home)
    order = pick(owned, cache_order, home_slot.astype(F32))
    tab_ref[0:1] = pack
    tab_ref[1:2] = pick(done & (prev == home), owner * SLOTS + pair_rank, cache_slot)
    tab_ref[2:3] = pack // NS * NR + pack % NS
    tab_ref[3:4] = order
    tab_ref[4:5] = order // SLOTS * 16 + order % SLOTS
    tab_ref[5:6] = pick(owned, home_slot, cache_order.astype(F32))
    tab_ref[6:7] = pick(owned, home_slot, jnp.ones((1, n), F32))
    tab_ref[7:8] = jnp.zeros((1, width), jnp.int32)


def shards(
    lm_query, lm_cache, language_new_pair, lm_lengths, lm_resid, lm_wo, lm_gain, lm_adapt,
    det_noise, det_pending, det_cache, det_qkv, det_out, det_gain, complete, owner, prev_owner,
):
    S, T, U = lax.axis_size("stream"), lax.axis_size("tensor"), lax.axis_size("sub")
    NP = T * U
    home = lax.axis_index("stream")
    NS = lm_query.shape[0]
    SH = NS * U
    NR = up(NS, 16)
    M = U * NR
    QW = lm_query.shape[1]
    KV = lm_cache.shape[-1] // HEAD_WIDTH
    R = QUERY_HEADS // KEY_VALUE_HEADS
    span = det_noise.shape[1]
    CW = det_noise.shape[2]
    TOK = up(span, 16)
    past = det_cache.shape[2]
    XR = up(2 * past, 128)
    SL = S * SLOTS
    CL = up(SL, 16)
    HID = lm_resid.shape[1]
    AW = lm_adapt.shape[1]

    n = owner.shape[0]
    tables = pl.pallas_call(
        functools.partial(routing_kernel, (S, SH, NS, NR)),
        out_shape=jax.ShapeDtypeStruct((8, up(SL, 128)), jnp.int32),
        compiler_params=pltpu.CompilerParams(vmem_limit_bytes=60 * 1024 * 1024),
    )(complete.reshape(1, n), owner.reshape(1, n), prev_owner.reshape(1, n))
    LR = 2 * lm_cache.shape[1]
    dcache = det_cache.reshape(SH, past, 2, CW)
    sizes = (S, T, U)
    V = pl.BlockSpec(memory_space=pltpu.VMEM)
    SM = pl.BlockSpec(memory_space=pltpu.SMEM)
    ANY = pl.BlockSpec(memory_space=pl.ANY)
    v = pltpu.VMEM
    dma = pltpu.SemaphoreType.DMA
    scratch = [
        v(lm_wo.shape, BF16), v(lm_adapt.shape, BF16), v(det_qkv.shape, BF16),
        v(det_out.shape, BF16), v((NS, 1, LR), F32), v((KV, NS, 8, HEAD_WIDTH), F32),
        v((M, HID), F32),
        v((SL, TOK, CW), BF16), v((SL, TOK, CW), BF16),
        v((SL, XR, CW), BF16), v((SL, XR, CW), BF16),
        v((U, NR, QW), BF16), v((T, M, HID), BF16), v((U, M, AW + 128), F32),
        v((M, CW), F32), v((S * 16, CW), F32), v((S, 16, CW), BF16), v((S, 16, CW), BF16),
        v((S * 16, CW), F32), v((NP, SL, TOK, CW), BF16), v((CL, CW), F32),
        v((NP, CL, CW), BF16), v((NP, CL, CW), F32), v((SL, TOK, NP * CW), BF16),
        v((SL, TOK, CW), BF16), v((SL, TOK, CW), BF16), v((SL, TOK, CW), BF16),
        v((SLOTS * TOK, CW), BF16), v((S, T, SLOTS * TOK, CW), F32),
        v((U - 1, S, T, SLOTS * TOK, CW), BF16), v((U - 1, S, T, SLOTS * TOK, CW), BF16),
        v((T - 1, S, SLOTS * TOK, CW), BF16), v((T - 1, S, SLOTS * TOK, CW), BF16),
        v((SL, TOK, CW), F32),
        dma((4,)), dma((S,)), dma((S,)), dma((S,)), dma((S,)), dma((S,)), dma((S,)),
        dma((U,)), dma((U,)), dma((T,)), dma((T,)), dma((U,)), dma((U,)),
        dma((T,)), dma((T,)), dma((U * T,)), dma((U * T,)), dma((NP,)), dma((NP,)),
        dma((U, S)), dma((U, S)), dma((T, S)), dma((T, S)),
    ]
    hidden, new_state = pl.pallas_call(
        functools.partial(kernel, sizes, past),
        out_shape=(
            jax.ShapeDtypeStruct((SH, HID), BF16),
            jax.ShapeDtypeStruct((SL, span, CW), BF16),
        ),
        in_specs=[SM] * 2 + [V] * 9 + [ANY] * 4,
        out_specs=(V, V),
        scratch_shapes=scratch,
        compiler_params=pltpu.CompilerParams(
            collective_id=0, has_side_effects=True, vmem_limit_bytes=60 * 1024 * 1024
        ),
    )(
        tables, lm_lengths, det_noise, det_pending, dcache, lm_query, lm_cache, language_new_pair,
        lm_resid, lm_gain.reshape(-1, 128), det_gain.reshape(-1, 128),
        lm_wo, lm_adapt, det_qkv, det_out,
    )
    return hidden, new_state.reshape(1, S, SLOTS, span, CW)


def solution(mesh):
    return jax.shard_map(
        shards,
        mesh=mesh,
        in_specs=(
            P(("groups", "stream", "sub"), "tensor"),
            P(("groups", "stream", "sub"), None, None, "tensor"),
            P(("groups", "stream", "sub"), None, "tensor"),
            P("groups"),
            P(("groups", "stream"), "sub"),
            P("tensor", "sub"),
            P("sub"),
            P("sub", "tensor"),
            P(("groups", "stream"), None, ("tensor", "sub")),
            P(("groups", "stream"), None, ("tensor", "sub")),
            P(("groups", "stream"), None, None, None, ("tensor", "sub")),
            P(None, None, ("tensor", "sub")),
            P(("tensor", "sub"), None),
            P(),
            P("groups"),
            P("groups"),
            P("groups"),
        ),
        out_specs=(
            P(("groups", "stream"), "sub"),
            P(("groups", "stream"), None, None, None, ("tensor", "sub")),
        ),
        check_vma=False,
    )
```

```python
import functools

import jax
import jax.numpy as jnp
from jax import lax
from jax.experimental import pallas as pl
from jax.experimental.pallas import tpu as pltpu
from jax.sharding import PartitionSpec as P

QUERY_HEADS = 28
KEY_VALUE_HEADS = 4
HEAD_WIDTH = 128
DHD = 64
SLOTS = 6
MESH = pl.DeviceIdType.MESH

step_size = 0.5
epsilon = 1e-06
NEG = -1e30
F32 = jnp.float32
BF16 = jnp.bfloat16


def up(n, m):
    return (n + m - 1) // m * m


def dot_nt(a, b):
    return lax.dot_general(a, b, (((1,), (1,)), ((), ())), preferred_element_type=F32)


def kernel(
    sizes,
    past_len,
    tab_ref, len_ref,
    noise_ref, pend_ref, dcache_ref, query_ref, lmx_ref, pair_ref, resid_ref, gain_ref, dgain_ref,
    wo_hbm, adapt_hbm, qkv_hbm, dout_hbm,
    hid_ref, out_ref,
    wo, adapt, qkv, dout, bias_s, q_s, resid_s,
    stsend, strecv, csend, crecv, att_all, parts, condx, condf, condpack, condsend, condrecv,
    condrf, gath, n29, lg, lgf, a_s, qb, kb, vb, mx, own, ocs, ocr, oxs, oxr, res,
    w_sem, st_s, st_r, ca_s, ca_r, co_s, co_r, at_s, at_r, pa_s, pa_r, cx_s, cx_r,
    g_s, g_r, gc_s, gc_r, l_s, l_r, oc_s, oc_r, o_s, o_r,
):
    S, T, U = sizes
    past = 2 * past_len
    NP = T * U
    me = lax.axis_index("stream")
    t_me = lax.axis_index("tensor")
    u_me = lax.axis_index("sub")
    p_me = t_me * U + u_me
    SL, TOK, CW = stsend.shape
    KV, NS = q_s.shape[0], q_s.shape[1]
    NR = att_all.shape[1]
    R = QUERY_HEADS // KEY_VALUE_HEADS
    last = out_ref.shape[1] - 1

    def row_of(ref):
        g = ref[...].astype(F32)
        return jnp.concatenate([g[i:i + 1] for i in range(g.shape[0])], axis=1)

    def at_stream(d):
        return {"stream": lax.rem(me + d, S)}

    def at_part(d):
        peer = lax.rem(p_me + d, NP)
        return {"tensor": lax.div(peer, U), "sub": lax.rem(peer, U)}

    def send(src, dst, ss, rs, dev):
        c = pltpu.make_async_remote_copy(
            src_ref=src, dst_ref=dst, send_sem=ss, recv_sem=rs, device_id=dev,
            device_id_type=MESH,
        )
        c.start()
        return c

    loads = []
    for i, (s, d) in enumerate(((wo_hbm, wo), (adapt_hbm, adapt), (qkv_hbm, qkv), (dout_hbm, dout))):
        c = pltpu.make_async_copy(s, d, w_sem.at[i])
        c.start()
        loads.append(c)

    barrier = pltpu.get_barrier_semaphore()
    for d in range(1, S):
        pl.semaphore_signal(barrier, inc=1, device_id=at_stream(d), device_id_type=MESH)
    for d in range(1, NP):
        pl.semaphore_signal(barrier, inc=1, device_id=at_part(d), device_id_type=MESH)

    def pack_state(i, _):
        k = tab_ref[0, i]
        pend = jnp.concatenate([pend_ref[k].astype(F32), jnp.zeros((1, CW), F32)], axis=0)
        row = noise_ref[k].astype(F32) + pend
        row = jnp.concatenate([row, jnp.zeros((TOK - last - 1, CW), F32)], axis=0)
        stsend[i] = row.astype(BF16)
        return 0

    lax.fori_loop(0, SL, pack_state, 0)
    pl.semaphore_wait(barrier, S - 1 + NP - 1)
    st_copies = []
    for d in range(1, S):
        o = lax.rem(me + d, S)
        st_copies.append(
            send(stsend.at[pl.ds(o * SLOTS, SLOTS)], strecv.at[pl.ds(me * SLOTS, SLOTS)],
                 st_s.at[d], st_r.at[d], at_stream(d))
        )

    if past < csend.shape[1]:
        csend[:, past:] = jnp.zeros((SL, csend.shape[1] - past, CW), BF16)

    def pack_cache(i, _):
        row = dcache_ref[tab_ref[1, i]].reshape(past, CW)
        csend[i, 0:past] = row
        return 0

    def pack_block(d):
        o = lax.rem(me + d, S)
        lax.fori_loop(o * SLOTS, o * SLOTS + SLOTS, pack_cache, 0)

    near = sorted(range(1, S), key=lambda d: (min(d, S - d), d))
    ca_copies = {}

    def send_cache(d):
        o = lax.rem(me + d, S)
        ca_copies[d] = send(
            csend.at[pl.ds(o * SLOTS, SLOTS)], crecv.at[pl.ds(me * SLOTS, SLOTS)],
            ca_s.at[d], ca_r.at[d], at_stream(d),
        )

    for d in near[:S // 2]:
        pack_block(d)
        send_cache(d)

    def keep_own(i, _):
        c = me * SLOTS + i
        strecv[c] = stsend[c]
        crecv[c] = csend[c]
        return 0


    scale = HEAD_WIDTH ** (-0.5)
    LR = bias_s.shape[2]
    lane_l = lax.broadcasted_iota(jnp.int32, (1, LR), 1)
    first = (me * U + u_me) * NS
    for i in range(NS):
        seen = (lane_l % 2 == 0) & (lane_l < 2 * len_ref[first + i])
        bias_s[i] = jnp.where(seen, 0.0, NEG)
    bias = bias_s[...]
    q_s[...] = jnp.zeros(q_s.shape, F32)
    for h in range(KV * R):
        q_s[h // R, :, h % R, :] = query_ref[
            :, h * HEAD_WIDTH:(h + 1) * HEAD_WIDTH
        ].astype(F32)
    if NR > NS:
        resid_s[...] = jnp.zeros(resid_s.shape, F32)
    for u in range(U):
        resid_s[u * NR:u * NR + NS] = resid_ref[...].astype(F32)[u * NS:(u + 1) * NS]
    pair = pair_ref[...].astype(F32)
    if NR > NS:
        att_all[u_me] = jnp.zeros(att_all.shape[1:], BF16)
    for kv in range(KV):
        q = q_s[kv]
        pair_kv = pair[:, :, kv * HEAD_WIDTH:(kv + 1) * HEAD_WIDTH]
        x = lmx_ref[:, :, :, kv * HEAD_WIDTH:(kv + 1) * HEAD_WIDTH].reshape(NS, LR, HEAD_WIDTH)
        s = lax.dot_general(q.astype(BF16), x, (((2,), (2,)), ((0,), (0,))), preferred_element_type=F32)
        s = s * scale + bias
        s_new = jnp.sum(q * pair_kv[:, 0:1], axis=-1, keepdims=True) * scale
        top = jnp.maximum(jnp.max(s, axis=-1, keepdims=True), s_new)
        w = jnp.exp(s - top)
        w_new = jnp.exp(s_new - top)
        total = jnp.sum(w, axis=-1, keepdims=True) + w_new
        w_rows = w.reshape(NS * 8, w.shape[2])
        w_odd = pltpu.roll(w_rows, 1, 1).astype(BF16).reshape(w.shape)
        o = lax.dot_general(w_odd, x, (((2,), (1,)), ((0,), (0,))), preferred_element_type=F32)
        o = o + w_new.astype(BF16).astype(F32) * pair_kv[:, 1:2]
        o = o / total
        for r in range(R):
            col = (kv * R + r) * HEAD_WIDTH
            att_all[u_me, 0:NS, col:col + HEAD_WIDTH] = o[:, r, :].astype(BF16)
    at_copies = []
    for d in range(1, U):
        at_copies.append(
            send(att_all.at[u_me], att_all.at[u_me], at_s.at[d], at_r.at[d],
                 {"sub": lax.rem(u_me + d, U)})
        )
    late = near[S // 2:]
    pack_block(0)
    lax.fori_loop(0, SLOTS, keep_own, 0)
    for d in late[:len(late) // 2]:
        pack_block(d)
    for c in at_copies:
        c.wait_recv()
    loads[0].wait()
    M = U * NR
    att = att_all[...].reshape(M, att_all.shape[2])
    parts[t_me] = jnp.dot(att, wo[...], preferred_element_type=F32).astype(BF16)
    pa_copies = []
    for d in range(1, T):
        pa_copies.append(
            send(parts.at[t_me], parts.at[t_me], pa_s.at[d], pa_r.at[d],
                 {"tensor": lax.rem(t_me + d, T)})
        )
    for d in late[len(late) // 2:]:
        pack_block(d)
    for c in st_copies:
        c.wait_recv()

    def arrange(c, _):
        row = strecv[tab_ref[3, c]]
        gath[p_me, c] = row
        n29[pl.ds(c, 1), :] = row.astype(F32)[last:last + 1, :]
        return 0

    lax.fori_loop(0, SL, arrange, 0)
    for c in pa_copies:
        c.wait_recv()
    g_copies, gc_copies = [], []

    def share(j, part):
        for e in range(1, U):
            i = (e - 1) * T + j
            gc_copies.append(
                send(gath.at[part], gath.at[part], gc_s.at[i], gc_r.at[i],
                     {"sub": lax.rem(u_me + e, U)})
            )

    for d in range(1, T):
        g_copies.append(
            send(gath.at[p_me], gath.at[p_me], g_s.at[d], g_r.at[d],
                 {"tensor": lax.rem(t_me + d, T)})
        )
    share(0, p_me)
    mixing = parts[0].astype(F32)
    for t in range(1, T):
        mixing = mixing + parts[t].astype(F32)
    hidden = (resid_s[...] + mixing).astype(BF16)
    for u in range(U):
        hid_ref[u * NS:(u + 1) * NS] = hidden[u * NR:u * NR + NS]
    wide = hidden.astype(F32)
    gained = (wide * row_of(gain_ref)).astype(BF16)
    loads[1].wait()
    AW = adapt.shape[1]
    condx[u_me, :, 0:AW] = jnp.dot(gained, adapt[...], preferred_element_type=F32)
    condx[u_me, :, AW:AW + 128] = jnp.broadcast_to(
        jnp.sum(wide * wide, axis=-1, keepdims=True), (M, 128)
    )
    cx_copies = []
    for d in range(1, U):
        cx_copies.append(
            send(condx.at[u_me], condx.at[u_me], cx_s.at[d], cx_r.at[d],
                 {"sub": lax.rem(u_me + d, U)})
        )
    condpack[...] = jnp.zeros(condpack.shape, F32)
    for c in cx_copies:
        c.wait_recv()
    mine = pl.ds(pl.multiple_of(u_me * CW, 128), CW)
    acc, sq = condx[0, :, mine], condx[0, :, AW:AW + 128]
    for u in range(1, U):
        acc = acc + condx[u, :, mine]
        sq = sq + condx[u, :, AW:AW + 128]
    inv = lax.rsqrt(sq[:, 0:1] / (hidden.shape[1] * U) + epsilon)
    condf[...] = acc * inv

    def pack_cond(o, _):
        for r in range(SLOTS):
            condpack[pl.ds(o * 16 + r, 1), :] = condf[pl.ds(tab_ref[2, o * SLOTS + r], 1), :]
        return 0

    lax.fori_loop(0, S, pack_cond, 0)
    condsend[...] = condpack[...].astype(BF16).reshape(condsend.shape)
    co_copies = []
    for d in range(1, S):
        o = lax.rem(me + d, S)
        co_copies.append(
            send(condsend.at[o], condrecv.at[me], co_s.at[d], co_r.at[d], at_stream(d))
        )
    for d in late:
        send_cache(d)
    condrecv[me] = condsend[me]
    lgf[...] = jnp.zeros(lgf.shape, F32)
    for d in range(1, T):
        g_copies[d - 1].wait_recv()
        share(d, lax.rem(t_me - d + T, T) * U + u_me)
    for c in co_copies:
        c.wait_recv()
    condrf[...] = condrecv[...].astype(F32).reshape(condrf.shape)

    def last_rows(c, _):
        lgf[p_me, pl.ds(c, 1), :] = n29[pl.ds(c, 1), :] + condrf[pl.ds(tab_ref[4, c], 1), :]
        return 0

    lax.fori_loop(0, SL, last_rows, 0)
    lg[p_me] = lgf[p_me].astype(BF16)
    l_copies = []
    for d in range(1, NP):
        l_copies.append(send(lg.at[p_me], lg.at[p_me], l_s.at[d], l_r.at[d], at_part(d)))
    for c in gc_copies:
        c.wait_recv()
    for c in l_copies:
        c.wait_recv()
    lgf[...] = lg[...].astype(F32)

    is_last = lax.broadcasted_iota(jnp.int32, (TOK, CW), 0) == last

    def full_rows(part, c):
        return jnp.where(is_last, lgf[part, pl.ds(c, 1), :], gath[part, c].astype(F32))

    dgain = row_of(dgain_ref)

    def normalize(c, _):
        rows = [full_rows(pt, c) for pt in range(NP)]
        ss = rows[0] * rows[0]
        for x in rows[1:]:
            ss = ss + x * x
        inv = lax.rsqrt(jnp.sum(ss, axis=-1, keepdims=True) / (NP * CW) + epsilon)
        for pt in range(NP):
            a_s[c, :, pt * CW:(pt + 1) * CW] = (
                rows[pt] * inv * dgain[:, pt * CW:(pt + 1) * CW]
            ).astype(BF16)
        return 0

    lax.fori_loop(0, SL, normalize, 0)
    loads[2].wait()
    loads[3].wait()

    def project(p, _):
        here = pl.ds(p * SLOTS, SLOTS)
        a = a_s[here].reshape(SLOTS * TOK, NP * CW)
        for k, dst in enumerate((qb, kb, vb)):
            y = jnp.dot(a, qkv[k], preferred_element_type=F32)
            if k == 0:
                y = y * (DHD ** (-0.5))
            dst[here] = y.astype(BF16).reshape(SLOTS, TOK, CW)
        return 0

    lax.fori_loop(0, S, project, 0)

    H = CW // DHD
    lane = lax.broadcasted_iota(jnp.int32, (1, CW), 1)
    heads = [(lane // DHD == h).astype(F32) for h in range(H)]
    heads_b = [m.astype(BF16) for m in heads]
    XR = crecv.shape[1]
    key_lane = lax.broadcasted_iota(jnp.int32, (1, XR), 1)
    bias_c = jnp.where((key_lane % 2 == 0) & (key_lane < past), 0.0, NEG)
    bias_o = jnp.where(lax.broadcasted_iota(jnp.int32, (1, TOK), 1) <= last, 0.0, NEG)

    o_copies = [[] for _ in range(S)]
    oc_copies = [[] for _ in range(S)]

    def across(d):
        for c in oc_copies[d]:
            c.wait_recv()
        for j in list(range(1, T)) + [0]:
            y = own[d, j]
            for e in range(1, U):
                y = y + ocr[e - 1, d, j].astype(F32)
            if j == 0:
                own[d, j] = y
            else:
                oxs[j - 1, d] = y.astype(BF16)
                o_copies[d].append(
                    send(oxs.at[j - 1, d], oxr.at[j - 1, d], o_s.at[j, d], o_r.at[j, d],
                         {"tensor": lax.rem(t_me + j, T)})
                )

    for d, shift in enumerate([0] + near):
        p = lax.rem(me - shift + S, S)
        if d > 0:
            ca_copies[shift].wait_recv()

        def attend(k, _):
            c = p * SLOTS + k
            q = qb[c]
            qs = jnp.concatenate([q * m for m in heads_b], axis=0)
            x = crecv[c]
            s = dot_nt(qs, x) + bias_c
            so = dot_nt(qs, kb[c]) + bias_o
            top = jnp.maximum(
                jnp.max(s, axis=-1, keepdims=True), jnp.max(so, axis=-1, keepdims=True)
            )
            w = jnp.exp(s - top)
            w_own = jnp.exp(so - top)
            total = jnp.sum(w, axis=-1, keepdims=True) + jnp.sum(w_own, axis=-1, keepdims=True)
            y = jnp.dot(pltpu.roll(w, 1, 1).astype(BF16), x, preferred_element_type=F32)
            y = y + jnp.dot(w_own.astype(BF16), vb[c], preferred_element_type=F32)
            y = y / total
            m = y[0:TOK] * heads[0]
            for h in range(1, H):
                m = m + y[h * TOK:(h + 1) * TOK] * heads[h]
            mx[pl.ds(pl.multiple_of(k * TOK, TOK), TOK), :] = m.astype(BF16)
            return 0

        lax.fori_loop(0, SLOTS, attend, 0, unroll=True)
        for e in range(U):
            u = lax.rem(u_me + e, U)
            for j in range(T):
                pt = lax.rem(t_me + j, T) * U + u
                y = jnp.dot(
                    mx[...], dout[:, pl.ds(pl.multiple_of(pt * CW, 128), CW)],
                    preferred_element_type=F32,
                )
                if e == 0:
                    own[d, j] = y
                else:
                    ocs[e - 1, d, j] = y.astype(BF16)
            if e > 0:
                oc_copies[d].append(
                    send(ocs.at[e - 1, d], ocr.at[e - 1, d], oc_s.at[e, d], oc_r.at[e, d], {"sub": u})
                )
        if d > 0:
            across(d - 1)
    across(S - 1)
    for d, shift in enumerate([0] + near):
        p = lax.rem(me - shift + S, S)
        mix = own[d, 0]
        for j in range(1, T):
            o_copies[d][j - 1].wait_recv()
            mix = mix + oxr[j - 1, d].astype(F32)
        mix = mix.reshape(SLOTS, TOK, CW)
        for k in range(SLOTS):
            c = p * SLOTS + k
            x = full_rows(p_me, c)
            res[c] = step_size * (x + mix[k])

    def write(qn, _):
        y = res[tab_ref[5, qn]] * tab_ref[6, qn].astype(F32)
        out_ref[qn] = y[0:last + 1, :].astype(BF16)
        return 0

    lax.fori_loop(0, SL, write, 0)
    for c in (sum(o_copies, []) + sum(oc_copies, []) + gc_copies + st_copies + list(ca_copies.values()) + at_copies + pa_copies + g_copies + cx_copies
              + co_copies + l_copies):
        c.wait_send()


def routing_kernel(dims, done_ref, owner_ref, prev_ref, tab_ref):
    S, SH, NS, NR = dims
    n = done_ref.shape[1]
    home = lax.axis_index("stream")
    done = done_ref[...] == 1
    owner = owner_ref[...]
    prev = prev_ref[...]
    before = lax.broadcasted_iota(jnp.int32, (n, n), 0)
    after = lax.broadcasted_iota(jnp.int32, (n, n), 1)
    earlier = (before < after).astype(F32)
    same = jnp.where(before // SH == after // SH, earlier, 0.0).astype(BF16)
    earlier = earlier.astype(BF16)

    def rank(key, count, valid, order):
        rows = lax.broadcasted_iota(jnp.int32, (count, n), 0)
        hot = jnp.where((rows == key) & valid, 1.0, 0.0)
        cum = jnp.dot(hot.astype(BF16), order, preferred_element_type=F32)
        return jnp.sum(cum * hot, axis=0, keepdims=True)

    always = owner >= 0
    home_rank = rank(owner, S, done, same)
    cache_slot = rank(prev, S, always, earlier)
    pair_rank = rank(prev * S + owner, S * S, done, earlier).astype(jnp.int32)
    ids = lax.broadcasted_iota(jnp.int32, (1, n), 1)
    shard = ids // SH
    local = (ids - shard * SH).astype(F32)
    home_slot = shard * SLOTS + home_rank.astype(jnp.int32)
    target = owner * SLOTS + home_rank.astype(jnp.int32)
    cache_order = prev * SLOTS + pair_rank
    width = tab_ref.shape[1]
    slots = lax.broadcasted_iota(jnp.int32, (width, n), 0)

    def pick(valid, slot, value):
        hot = jnp.where((slots == slot) & valid, 1.0, 0.0).astype(BF16)
        value = jnp.broadcast_to(value, (8, n)).astype(BF16)
        return dot_nt(value, hot)[0:1].astype(jnp.int32)

    pack = pick(done & (shard == home), target, local)
    owned = done & (owner == home)
    order = pick(owned, cache_order, home_slot.astype(F32))
    tab_ref[0:1] = pack
    tab_ref[1:2] = pick(done & (prev == home), owner * SLOTS + pair_rank, cache_slot)
    tab_ref[2:3] = pack // NS * NR + pack % NS
    tab_ref[3:4] = order
    tab_ref[4:5] = order // SLOTS * 16 + order % SLOTS
    tab_ref[5:6] = pick(owned, home_slot, cache_order.astype(F32))
    tab_ref[6:7] = pick(owned, home_slot, jnp.ones((1, n), F32))
    tab_ref[7:8] = jnp.zeros((1, width), jnp.int32)


def shards(
    lm_query, lm_cache, language_new_pair, lm_lengths, lm_resid, lm_wo, lm_gain, lm_adapt,
    det_noise, det_pending, det_cache, det_qkv, det_out, det_gain, complete, owner, prev_owner,
):
    S, T, U = lax.axis_size("stream"), lax.axis_size("tensor"), lax.axis_size("sub")
    NP = T * U
    home = lax.axis_index("stream")
    NS = lm_query.shape[0]
    SH = NS * U
    NR = up(NS, 16)
    M = U * NR
    QW = lm_query.shape[1]
    KV = lm_cache.shape[-1] // HEAD_WIDTH
    R = QUERY_HEADS // KEY_VALUE_HEADS
    span = det_noise.shape[1]
    CW = det_noise.shape[2]
    TOK = up(span, 16)
    past = det_cache.shape[2]
    XR = up(2 * past, 128)
    SL = S * SLOTS
    CL = up(SL, 16)
    HID = lm_resid.shape[1]
    AW = lm_adapt.shape[1]

    n = owner.shape[0]
    tables = pl.pallas_call(
        functools.partial(routing_kernel, (S, SH, NS, NR)),
        out_shape=jax.ShapeDtypeStruct((8, up(SL, 128)), jnp.int32),
        compiler_params=pltpu.CompilerParams(vmem_limit_bytes=60 * 1024 * 1024),
    )(complete.reshape(1, n), owner.reshape(1, n), prev_owner.reshape(1, n))
    LR = 2 * lm_cache.shape[1]
    dcache = det_cache.reshape(SH, past, 2, CW)
    sizes = (S, T, U)
    V = pl.BlockSpec(memory_space=pltpu.VMEM)
    SM = pl.BlockSpec(memory_space=pltpu.SMEM)
    ANY = pl.BlockSpec(memory_space=pl.ANY)
    v = pltpu.VMEM
    dma = pltpu.SemaphoreType.DMA
    scratch = [
        v(lm_wo.shape, BF16), v(lm_adapt.shape, BF16), v(det_qkv.shape, BF16),
        v(det_out.shape, BF16), v((NS, 1, LR), F32), v((KV, NS, 8, HEAD_WIDTH), F32),
        v((M, HID), F32),
        v((SL, TOK, CW), BF16), v((SL, TOK, CW), BF16),
        v((SL, XR, CW), BF16), v((SL, XR, CW), BF16),
        v((U, NR, QW), BF16), v((T, M, HID), BF16), v((U, M, AW + 128), F32),
        v((M, CW), F32), v((S * 16, CW), F32), v((S, 16, CW), BF16), v((S, 16, CW), BF16),
        v((S * 16, CW), F32), v((NP, SL, TOK, CW), BF16), v((CL, CW), F32),
        v((NP, CL, CW), BF16), v((NP, CL, CW), F32), v((SL, TOK, NP * CW), BF16),
        v((SL, TOK, CW), BF16), v((SL, TOK, CW), BF16), v((SL, TOK, CW), BF16),
        v((SLOTS * TOK, CW), BF16), v((S, T, SLOTS * TOK, CW), F32),
        v((U - 1, S, T, SLOTS * TOK, CW), BF16), v((U - 1, S, T, SLOTS * TOK, CW), BF16),
        v((T - 1, S, SLOTS * TOK, CW), BF16), v((T - 1, S, SLOTS * TOK, CW), BF16),
        v((SL, TOK, CW), F32),
        dma((4,)), dma((S,)), dma((S,)), dma((S,)), dma((S,)), dma((S,)), dma((S,)),
        dma((U,)), dma((U,)), dma((T,)), dma((T,)), dma((U,)), dma((U,)),
        dma((T,)), dma((T,)), dma((U * T,)), dma((U * T,)), dma((NP,)), dma((NP,)),
        dma((U, S)), dma((U, S)), dma((T, S)), dma((T, S)),
    ]
    hidden, new_state = pl.pallas_call(
        functools.partial(kernel, sizes, past),
        out_shape=(
            jax.ShapeDtypeStruct((SH, HID), BF16),
            jax.ShapeDtypeStruct((SL, span, CW), BF16),
        ),
        in_specs=[SM] * 2 + [V] * 9 + [ANY] * 4,
        out_specs=(V, V),
        scratch_shapes=scratch,
        compiler_params=pltpu.CompilerParams(
            collective_id=0, has_side_effects=True, vmem_limit_bytes=60 * 1024 * 1024
        ),
    )(
        tables, lm_lengths, det_noise, det_pending, dcache, lm_query, lm_cache, language_new_pair,
        lm_resid, lm_gain.reshape(-1, 128), det_gain.reshape(-1, 128),
        lm_wo, lm_adapt, det_qkv, det_out,
    )
    return hidden, new_state.reshape(1, S, SLOTS, span, CW)


def solution(mesh):
    return jax.shard_map(
        shards,
        mesh=mesh,
        in_specs=(
            P(("groups", "stream", "sub"), "tensor"),
            P(("groups", "stream", "sub"), None, None, "tensor"),
            P(("groups", "stream", "sub"), None, "tensor"),
            P("groups"),
            P(("groups", "stream"), "sub"),
            P("tensor", "sub"),
            P("sub"),
            P("sub", "tensor"),
            P(("groups", "stream"), None, ("tensor", "sub")),
            P(("groups", "stream"), None, ("tensor", "sub")),
            P(("groups", "stream"), None, None, None, ("tensor", "sub")),
            P(None, None, ("tensor", "sub")),
            P(("tensor", "sub"), None),
            P(),
            P("groups"),
            P("groups"),
            P("groups"),
        ),
        out_specs=(
            P(("groups", "stream"), "sub"),
            P(("groups", "stream"), None, None, None, ("tensor", "sub")),
        ),
        check_vma=False,
    )
```
